512 devices in a mesh: row: 32 (over y, x), col: 16 (over z, core).
Axes of the slice: x: 4, y: 8, z: 8, core: 2. Of those that a mesh axis runs over, the one named last changes fastest.
Arguments:
- transition: float32 [16384, 16384], P('row', 'col'), may hold values from 0.1 to 10
- alphas: float32 [2, 256, 16384], P(None, 'col', 'row'), may hold values from 0.1 to 10
- beta_last: float32 [256, 16384], P('col', 'row'), may hold values from 0.1 to 10
- emission: float32 [128, 16384], P(None, 'row'), may hold values from 0.05 to 1
- token_ids: int32 [2, 256], P(None, 'col'), may hold values from 0 to 127
Outputs:
- beta_first: float32 [256, 16384], P('col', 'row')
- counts: float32 [16384, 16384], P('row', 'col')
The draws below stay inside these ranges and needn't reach their ends.
All inputs are finite; a program needn't handle non-finite values.
Results may differ from the reference program's by a relative error of at most 0.0001.
Values sent between devices are 32-bit elements; how exact they have to be, the bound alone decides.
A program may use at most 64 MiB of HBM per device.

```python
import math
import jax
import jax.numpy as jnp
from jax import lax

H = 16384
NCOL = 128
STEPS = 2
SEQ = 256


def place_ends(array, rng, low, top_value):
    spot = [jax.random.randint(jax.random.fold_in(rng, axis), (), 0, length) for axis, length in enumerate(array.shape)]
    longest = array.shape.index(max(array.shape))
    next_to = spot[:longest] + [(spot[longest] + 1) % array.shape[longest]] + spot[longest + 1:]
    return array.at[tuple(spot)].set(low).at[tuple(next_to)].set(top_value)


def levels(own_key, shape, split, low, largest):
    def one(position, parts):
        steps = jax.random.uniform(jax.random.fold_in(jax.random.fold_in(own_key, 6), position), (parts,), jnp.float32, low / len(split), largest / len(split))
        return jnp.repeat(jnp.exp(steps), shape[position] // parts).reshape((-1,) + (1,) * (len(shape) - position - 1))

    factor_of = one(*split[0])
    for cut in split[1:]:
        factor_of = factor_of * one(*cut)
    return factor_of


def setup_inputs(seed: int = 0) -> dict:
    arg_keys = jax.random.split(jax.random.key(seed), 6)
    return {
        "transition": jnp.clip(jnp.exp(math.log(10.0) - 4.6051702 * jax.random.uniform(arg_keys[0], (H, H), jnp.float32) ** levels(arg_keys[0], (H, H), ((0, 32), (1, 16)), -0.2, 0.2)), 0.1, 10.0),
        "alphas": jnp.clip(jnp.exp(math.log(10.0) - 4.6051702 * jax.random.uniform(arg_keys[1], (STEPS, SEQ, H), jnp.float32) ** levels(arg_keys[1], (STEPS, SEQ, H), ((1, 16), (2, 32)), -0.2, 0.2)), 0.1, 10.0),
        "beta_last": jnp.clip(jnp.exp(math.log(10.0) - 4.6051702 * jax.random.uniform(arg_keys[2], (SEQ, H), jnp.float32) ** levels(arg_keys[2], (SEQ, H), ((0, 16), (1, 32)), -0.2, 0.2)), 0.1, 10.0),
        "emission": jnp.clip(jnp.exp(math.log(1.0) - 2.9957323 * jax.random.uniform(arg_keys[3], (NCOL, H), jnp.float32) ** levels(arg_keys[3], (NCOL, H), ((1, 32),), -0.2, 0.2)), 0.05, 1.0),
        "token_ids": place_ends(jax.random.randint(arg_keys[4], (STEPS, SEQ), 0, NCOL), jax.random.fold_in(arg_keys[4], 1), 0, NCOL - 1).astype(jnp.int32),
    }


def reference(transition, alphas, beta_last, emission, token_ids):
    beta = beta_last
    total = jnp.zeros((H, H), jnp.float32)
    for k in range(STEPS):
        emit = emission[token_ids[k]]
        weighted = emit * beta
        u = jnp.dot(weighted, transition.T, precision=lax.Precision.HIGHEST, preferred_element_type=jnp.float32)
        z = jnp.sum(alphas[k] * u, axis=1)
        beta = (u / z[:, None]) * H
        scaled = alphas[k] / z[:, None]
        total = total + jnp.dot(scaled.T, weighted, precision=lax.Precision.HIGHEST, preferred_element_type=jnp.float32)
    factor = float(H * H) / float(SEQ * STEPS)
    counts = (transition * total) * factor
    return beta, counts
```

```python
import functools

import jax
import jax.numpy as jnp
from jax import lax
from jax.experimental import pallas as pl
from jax.experimental.pallas import tpu as pltpu
from jax.sharding import PartitionSpec as P

H = 16384
STEPS = 2
SEQ = 256
X, Y, Z, C = 4, 8, 8, 2
BS = SEQ // (Z * C)
HALF = BS * Z
RB = H // (X * Y)
CB = H // (Z * C)
NCOL = 128
FACTOR = float(H * H) / float(SEQ * STEPS)
F32 = jnp.float32
BF16 = jnp.bfloat16
MESH = pl.DeviceIdType.MESH


def loop(n, body, start=0):
    def step(i, carry):
        body(i)
        return carry

    lax.fori_loop(start, n, step, 0)


def remote(src, dst, send, recv, row, col):
    return pltpu.make_async_remote_copy(
        src_ref=src, dst_ref=dst, send_sem=send, recv_sem=recv, device_id=(row, col), device_id_type=MESH
    )


def wait(ref, sem):
    pltpu.make_async_copy(ref, ref, sem).wait()


def near_first(j):
    return (j % 2) * ((j + 1) // 2) + (1 - j % 2) * (8 - j // 2)


def split(v):
    hi = v.astype(BF16)
    return hi, (v - hi.astype(F32)).astype(BF16)


def dot(a, b, dims):
    return lax.dot_general(a, b, (dims, ((), ())), preferred_element_type=F32)


NT = ((1,), (1,))
NN = ((1,), (0,))


def kernel(
    trans_hbm, alphas_hbm, beta_hbm, emis_hbm, tok_ref,
    beta_out, counts_hbm,
    t_f, t_hi, t_lo, emis, beta0, al, at_hi, at_lo, tsend, tw, wblk, w, ub, pr, cr, tot, outb, zz, zy, zx, zp, zc,
    ld, t_s, t_r, a_s, a_r, ap, y_s, y_r, x_s, x_r, f_s, p_s, p_r, c_s, c_r, zz_s, zz_r, zy_s, zy_r, zx_s, zx_r, zp_s, zp_r, o_s,
):
    row = lax.axis_index("row")
    col = lax.axis_index("col")
    x, y, z, k = row % X, row // X, col // C, col % C
    kd = x // 2
    slot = x % 2
    q = (x - 2 * k + 4) % 4
    fslot = 1 - slot
    fhalf = q // 2
    fplus = ((q + 1) // 2) % 2
    xp, xm = (x + 1) % X, (x + X - 1) % X
    fx = fplus * xp + (1 - fplus) * xm
    other = z * C + 1 - k

    loads = [
        pltpu.make_async_copy(emis_hbm, emis, ld.at[0]),
        pltpu.make_async_copy(beta_hbm, beta0, ld.at[1]),
        pltpu.make_async_copy(alphas_hbm, al.at[:, pl.ds(k * HALF + z * BS, BS)], ld.at[2]),
        pltpu.make_async_copy(trans_hbm, t_f, ld.at[3]),
    ]
    for c in loads:
        c.start()

    bar = pltpu.get_barrier_semaphore()

    def greet(r, c):
        pl.semaphore_signal(bar, inc=1, device_id=(r, c), device_id_type=MESH)

    def greet_lines(d):
        greet(row, ((z + d) % Z) * C + k)
        greet(((y + d) % Y) * X + x, col)
        greet(((y + d) % Y) * X + x, other)

    loop(Z, greet_lines, 1)
    loop(X, lambda d: greet(y * X + (x + d) % X, col), 1)
    greet(row, other)

    @pl.when(y != z)
    def _():
        def greet_cross(d):
            greet(((y + d) % Y) * X + x, y * C + k)

            @pl.when((z + d) % Z != y)
            def _():
                greet(z * X + x, ((z + d) % Z) * C + k)

        loop(Z, greet_cross, 1)

    loads[0].wait()
    labels = lax.broadcasted_iota(jnp.int32, (NCOL, BS), 0)
    em = emis[...]

    def emit(step):
        onehot = (labels == tok_ref[step : step + 1, :]).astype(F32)
        return lax.dot_general(
            onehot, em, (((0,), (0,)), ((), ())), precision=lax.Precision.HIGHEST, preferred_element_type=F32
        )

    loads[1].wait()
    tsend[0] = emit(0) * beta0[...]
    tsend[1] = emit(1)

    apart = ((y - z + Z) % Z + Z - 1) // Z
    pl.semaphore_wait(bar, 3 * (Z - 1) + X + apart * (2 * Z - 3))

    for i in range(2):
        @pl.when(y != z)
        def _():
            remote(tsend.at[i], tw.at[i], t_s.at[i], t_r.at[i], z * X + x, y * C + k).start()

        @pl.when(y == z)
        def _():
            pltpu.make_async_copy(tsend.at[i], tw.at[i], t_r.at[i]).start()

    loads[2].wait()
    mine = al.at[:, pl.ds(k * HALF + z * BS, BS)]

    def alpha_send(d):
        remote(mine, mine, a_s.at[d], a_r.at[z], row, ((z + d) % Z) * C + k).start()

    loop(Z, alpha_send, 1)

    def rows(g, s):
        return pl.ds(g * HALF + s * BS, BS)

    def y_sends(step, src):
        dst = w.at[step, slot, rows(k, y)]

        @pl.when(k == kd)
        def _():
            pltpu.make_async_copy(src, dst, y_r.at[step, k, y]).start()

        @pl.when(k != kd)
        def _():
            remote(src, dst, y_s.at[step, 0], y_r.at[step, k, y], row, other).start()

        def send(j):
            to = (y + near_first(j)) % Y
            remote(src, dst, y_s.at[step, j], y_r.at[step, k, y], to * X + x, z * C + kd).start()

        loop(Y, send, 1)

    def x_sends(step, g):
        @pl.when(k == kd)
        def _():
            def send(j):
                s = (y + near_first(j)) % Y
                ref = w.at[step, slot, rows(g, s)]
                wait(ref, y_r.at[step, g, s])
                remote(ref, ref, x_s.at[step, 0, g, j], x_r.at[step, slot, g, s], y * X + xp, col).start()
                remote(ref, ref, x_s.at[step, 1, g, j], x_r.at[step, slot, g, s], y * X + xm, col).start()

            loop(Y, send)

    def forwards(step, g):
        def send(i):
            s = (y + near_first(2 * i + fhalf)) % Y
            ref = w.at[step, fslot, rows(g, s)]
            wait(ref, x_r.at[step, fslot, g, s])
            remote(ref, ref, f_s.at[step, g, i], x_r.at[step, fslot, g, s], y * X + fx, col).start()

        loop(Y // 2, send)

    def arrivals(step, g):
        def rest(i):
            s = (y + near_first(2 * i + 1 - fhalf)) % Y
            wait(w.at[step, fslot, rows(g, s)], x_r.at[step, fslot, g, s])

        loop(Y // 2, rest)

        @pl.when(k != kd)
        def _():
            def full(s):
                wait(w.at[step, slot, rows(g, s)], x_r.at[step, slot, g, s])

            loop(Y, full)

    def z_sum(buf, n):
        v = buf[0]
        for i in range(1, n):
            v = v + buf[i]
        return v

    def z_first(step, prod):
        part = prod[:, 0:128]
        for i in range(1, RB // 128):
            part = part + prod[:, i * 128 : (i + 1) * 128]
        zz[step, z] = jnp.broadcast_to(jnp.sum(jnp.transpose(part), axis=0, keepdims=True), (8, HALF))

        def send(d):
            ref = zz.at[step, z]
            remote(ref, ref, zz_s.at[step, d], zz_r.at[step, z], row, ((z + d) % Z) * C + k).start()

        loop(Z, send, 1)

    def z_second(step):
        loop(Z, lambda d: wait(zz.at[step, (z + d) % Z], zz_r.at[step, (z + d) % Z]), 1)
        zy[step, y] = z_sum(zz.at[step], Z)

        def send(d):
            ref = zy.at[step, y]
            remote(ref, ref, zy_s.at[step, d], zy_r.at[step, y], ((y + d) % Y) * X + x, col).start()

        loop(Y, send, 1)

    def z_third(step):
        loop(Y, lambda d: wait(zy.at[step, (y + d) % Y], zy_r.at[step, (y + d) % Y]), 1)
        zx[step, x] = z_sum(zy.at[step], Y)

        def send(d):
            ref = zx.at[step, x]
            remote(ref, ref, zx_s.at[step, d], zx_r.at[step, x], y * X + (x + d) % X, col).start()

        loop(X, send, 1)

    def z_fourth(step):
        loop(X, lambda d: wait(zx.at[step, (x + d) % X], zx_r.at[step, (x + d) % X]), 1)
        zp[step, k] = z_sum(zx.at[step], X)
        ref = zp.at[step, k]
        remote(ref, ref, zp_s.at[step], zp_r.at[step], row, other).start()

    def z_last(step):
        wait(zp.at[step, 1 - k], zp_r.at[step])
        for g in range(C):
            zc[step, g] = jnp.transpose(jnp.broadcast_to(zp[step, g, 0:1, :], (HALF, HALF)))

    def product(step, g):
        acc = None
        for sl in range(2):
            hi, lo = split(w[step, sl, g * HALF : (g + 1) * HALF, :])
            cols = slice(sl * RB, (sl + 1) * RB)
            both = dot(jnp.concatenate([hi, lo], axis=0), t_hi[:, cols], NT)
            part = both[:HALF] + both[HALF:] + dot(hi, t_lo[:, cols], NT)
            acc = part if acc is None else acc + part
        ub[step, g] = acc

        @pl.when(k != g)
        def _():
            remote(ub.at[step, g], pr.at[step], p_s.at[step], p_r.at[step], row, other).start()

        @pl.when(k == g)
        def _():
            wait(pr.at[step], p_r.at[step])
            u = ub[step, g] + pr[step]
            ub[step, g] = u

            def send(d):
                if step == 0:
                    s = (y + d) % Y
                    r, c = s * X + x, y * C + k
                else:
                    s = (z + d) % Z
                    r, c = row, s * C + k
                src = ub.at[step, g, pl.ds(s * BS, BS)]
                remote(src, cr.at[step, z], c_s.at[step, d], c_r.at[step, z], r, c).start()

            loop(Z, send, 1)
            if step == 0:
                src = ub.at[step, g, pl.ds(y * BS, BS)]

                @pl.when(y != z)
                def _():
                    remote(src, cr.at[step, z], c_s.at[step, 0], c_r.at[step, z], row, y * C + k).start()

                @pl.when(y == z)
                def _():
                    pltpu.make_async_copy(src, cr.at[step, z], c_r.at[step, z]).start()

                loop(Z, lambda d: wait(al.at[:, pl.ds(k * HALF + ((z + d) % Z) * BS, BS)], a_r.at[(z + d) % Z]), 1)
                half = al.at[:, pl.ds(k * HALF, HALF)]
                remote(half, half, ap.at[0], ap.at[1], row, other).start()
            else:
                src = ub.at[step, g, pl.ds(z * BS, BS)]
                pltpu.make_async_copy(src, cr.at[step, z], c_r.at[step, z]).start()
            z_first(step, u * al[step, pl.ds(k * HALF, HALF), :])

    def reduced(step):
        acc = None
        for i in range(Z):
            wait(cr.at[step, i], c_r.at[step, i])
            acc = cr[step, i] if acc is None else acc + cr[step, i]
        return acc

    def next_weighted(g):
        @pl.when(k == g)
        def _():
            wblk[...] = reduced(0) * tw[1]
            y_sends(1, wblk)

    def scaled_columns(step, sl):
        parts = []
        for g in range(C):
            inv = 1.0 / zc[step, g]
            parts.append(w[step, sl, g * HALF : (g + 1) * HALF, :] * jnp.concatenate([inv] * (RB // HALF), axis=1))
        return split(jnp.concatenate(parts, axis=0))

    def counts_part(step, hi, lo, r):
        return (
            dot(at_hi[step, r, :], hi, NN) + dot(at_lo[step, r, :], hi, NN) + dot(at_hi[step, r, :], lo, NN)
        )

    wait(tw.at[0], t_r.at[0])
    y_sends(0, tw.at[0])
    loads[3].wait()

    def split_rows(i):
        r = pl.ds(pl.multiple_of(i * 64, 64), 64)
        hi, lo = split(t_f[r, :])
        t_hi[r, :] = hi
        t_lo[r, :] = lo

    loop(RB // 64, split_rows)
    wait(tw.at[1], t_r.at[1])
    x_sends(0, 0)
    x_sends(0, 1)
    forwards(0, 0)
    arrivals(0, 0)
    product(0, 0)
    forwards(0, 1)
    arrivals(0, 1)
    product(0, 1)

    next_weighted(0)
    z_second(0)
    x_sends(1, 0)
    next_weighted(1)
    forwards(1, 0)
    z_third(0)
    wait(al.at[:, pl.ds((1 - k) * HALF, HALF)], ap.at[1])
    for step in range(STEPS):
        for i in range(RB // 128):
            hi, lo = split(jnp.transpose(al[step, :, i * 128 : (i + 1) * 128]))
            at_hi[step, i * 128 : (i + 1) * 128, :] = hi
            at_lo[step, i * 128 : (i + 1) * 128, :] = lo
    z_fourth(0)
    x_sends(1, 1)
    z_last(0)
    for sl in range(2):
        hi, lo = scaled_columns(0, sl)
        tot[:, sl * RB : (sl + 1) * RB] = counts_part(0, hi, lo, slice(None))
    arrivals(1, 0)
    product(1, 0)
    forwards(1, 1)
    arrivals(1, 1)
    product(1, 1)

    z_second(1)
    z_third(1)
    z_fourth(1)
    z_last(1)
    for sl in range(2):
        hi, lo = scaled_columns(1, sl)
        cols = slice(sl * RB, (sl + 1) * RB)
        outb[:, cols] = (t_f[:, cols] * (tot[:, cols] + counts_part(1, hi, lo, slice(None)))) * FACTOR
        pltpu.make_async_copy(outb.at[:, cols], counts_hbm.at[:, cols], o_s.at[sl]).start()
    norm = zc[1, k, pl.ds(pl.multiple_of(z * BS, BS), BS), :]
    beta_out[...] = (reduced(1) / jnp.concatenate([norm] * (RB // HALF), axis=1)) * float(H)

    @pl.when(y != z)
    def _():
        wait(tsend.at[0], t_s.at[0])
        wait(tsend.at[1], t_s.at[1])
        wait(cr.at[0, 0], c_s.at[0, 0])

    @pl.when(k != kd)
    def _():
        wait(wblk, y_s.at[0, 0])
        wait(wblk, y_s.at[1, 0])

    @pl.when(k == kd)
    def _():
        for step in range(STEPS):
            def sent(j):
                for g in range(C):
                    for d in range(2):
                        wait(wblk, x_s.at[step, d, g, j])

            loop(Y, sent)

    def sent_lines(d):
        wait(mine, a_s.at[d])
        for step in range(STEPS):
            wait(wblk, y_s.at[step, d])
            wait(wblk, c_s.at[step, d])
            wait(zz.at[0, 0], zz_s.at[step, d])
            wait(zz.at[0, 0], zy_s.at[step, d])

    loop(Z, sent_lines, 1)
    wait(al.at[:, pl.ds(0, HALF)], ap.at[0])
    for step in range(STEPS):
        wait(pr.at[0], p_s.at[step])
        wait(zz.at[0, 0], zp_s.at[step])
        loop(X, lambda d: wait(zz.at[0, 0], zx_s.at[step, d]), 1)

        def sent_on(i):
            for g in range(C):
                wait(wblk, f_s.at[step, g, i])

        loop(Y // 2, sent_on)
    for sl in range(2):
        cols = slice(sl * RB, (sl + 1) * RB)
        wait(outb.at[:, cols], o_s.at[sl])


def per_device(transition, alphas, beta_last, emission, token_ids):
    anywhere = pl.BlockSpec(memory_space=pl.ANY)
    vmem = pl.BlockSpec(memory_space=pltpu.VMEM)
    dma = pltpu.SemaphoreType.DMA
    return pl.pallas_call(
        kernel,
        out_shape=(
            jax.ShapeDtypeStruct((BS, RB), F32),
            jax.ShapeDtypeStruct((RB, CB), F32),
        ),
        in_specs=[anywhere] * 4 + [vmem],
        out_specs=(vmem, anywhere),
        scratch_shapes=[
            pltpu.VMEM((RB, CB), F32),
            pltpu.VMEM((RB, CB), BF16),
            pltpu.VMEM((RB, CB), BF16),
            pltpu.VMEM((NCOL, RB), F32),
            pltpu.VMEM((BS, RB), F32),
            pltpu.VMEM((STEPS, SEQ, RB), F32),
            pltpu.VMEM((STEPS, RB, SEQ), BF16),
            pltpu.VMEM((STEPS, RB, SEQ), BF16),
            pltpu.VMEM((2, BS, RB), F32),
            pltpu.VMEM((2, BS, RB), F32),
            pltpu.VMEM((BS, RB), F32),
            pltpu.VMEM((STEPS, 2, SEQ, RB), F32),
            pltpu.VMEM((STEPS, C, HALF, RB), F32),
            pltpu.VMEM((STEPS, HALF, RB), F32),
            pltpu.VMEM((STEPS, Z, BS, RB), F32),
            pltpu.VMEM((RB, CB), F32),
            pltpu.VMEM((RB, CB), F32),
            pltpu.VMEM((STEPS, Z, 8, HALF), F32),
            pltpu.VMEM((STEPS, Y, 8, HALF), F32),
            pltpu.VMEM((STEPS, X, 8, HALF), F32),
            pltpu.VMEM((STEPS, C, 8, HALF), F32),
            pltpu.VMEM((STEPS, C, HALF, HALF), F32),
            dma((4,)),
            dma((2,)), dma((2,)),
            dma((Z,)), dma((Z,)),
            dma((2,)),
            dma((STEPS, Y)), dma((STEPS, C, Y)),
            dma((STEPS, 2, C, Y)), dma((STEPS, 2, C, Y)),
            dma((STEPS, C, Y // 2)),
            dma((STEPS,)), dma((STEPS,)),
            dma((STEPS, Z)), dma((STEPS, Z)),
            dma((STEPS, Z)), dma((STEPS, Z)),
            dma((STEPS, Y)), dma((STEPS, Y)),
            dma((STEPS, X)), dma((STEPS, X)),
            dma((STEPS,)), dma((STEPS,)),
            dma((2,)),
        ],
        compiler_params=pltpu.CompilerParams(
            collective_id=0, has_side_effects=True, vmem_limit_bytes=48 * 1024 * 1024
        ),
    )(transition, alphas, beta_last, emission, token_ids)


def solution(mesh):
    return jax.shard_map(
        per_device,
        mesh=mesh,
        in_specs=(
            P("row", "col"),
            P(None, "col", "row"),
            P("col", "row"),
            P(None, "row"),
            P(None, "col"),
        ),
        out_specs=(P("col", "row"), P("row", "col")),
        check_vma=False,
    )
```

```python
import jax
import jax.numpy as jnp
from jax import lax
from jax.experimental import pallas as pl
from jax.experimental.pallas import tpu as pltpu
from jax.sharding import PartitionSpec as P

H = 16384
STEPS = 2
SEQ = 256
X, Y, Z, C = 4, 8, 8, 2
G = 2
BS = SEQ // (Z * C)
T = BS // G
HALF = SEQ // G
RB = H // (X * Y)
CB = H // (Z * C)
NCOL = 128
FACTOR = float(H * H) / float(SEQ * STEPS)
F32 = jnp.float32
BF16 = jnp.bfloat16
MESH = pl.DeviceIdType.MESH
NT = ((1,), (1,))
NN = ((1,), (0,))


def loop(n, body, start=0):
    def step(i, carry):
        body(i)
        return carry

    lax.fori_loop(start, n, step, 0)


def remote(src, dst, send, recv, row, col):
    return pltpu.make_async_remote_copy(
        src_ref=src, dst_ref=dst, send_sem=send, recv_sem=recv, device_id=(row, col), device_id_type=MESH
    )


def wait(ref, sem):
    pltpu.make_async_copy(ref, ref, sem).wait()


def near_first(j):
    return (j % 2) * ((j + 1) // 2) + (1 - j % 2) * (8 - j // 2)


def split(v):
    hi = v.astype(BF16)
    return hi, (v - hi.astype(F32)).astype(BF16)


def dot(a, b, dims):
    return lax.dot_general(a, b, (dims, ((), ())), preferred_element_type=F32)


def kernel(
    trans_hbm, alphas_hbm, beta_hbm, emis_hbm, tok_hbm,
    beta_out, counts_out,
    t_f, t_hi, t_lo, emis, beta0, tok, al, at_hi, at_lo, tsend, tw, wblk, w, ub, pr, cr, zpart, zz, zy, zx, zc,
    ld, t_s, t_r, a_s, a_r, ap, y_s, y_r, x_s, x_r, f_s, p_s, p_r, c_s, c_r, z_s, z_r,
):
    row = lax.axis_index("row")
    col = lax.axis_index("col")
    x, y, z, k = row % X, row // X, col // C, col % C
    kd = x // 2
    slot = x % 2
    q = (x - 2 * k + 4) % 4
    fslot = 1 - slot
    fhalf = q // 2
    fplus = ((q + 1) // 2) % 2
    xp, xm = (x + 1) % X, (x + X - 1) % X
    fx = fplus * xp + (1 - fplus) * xm
    other = z * C + 1 - k

    loads = [
        pltpu.make_async_copy(tok_hbm, tok, ld.at[0]),
        pltpu.make_async_copy(emis_hbm, emis, ld.at[1]),
        pltpu.make_async_copy(beta_hbm, beta0, ld.at[2]),
        pltpu.make_async_copy(alphas_hbm, al.at[:, :, z, k], ld.at[3]),
        pltpu.make_async_copy(trans_hbm, t_f, ld.at[4]),
    ]
    for c in loads:
        c.start()

    bar = pltpu.get_barrier_semaphore()

    def greet(r, c):
        pl.semaphore_signal(bar, inc=1, device_id=(r, c), device_id_type=MESH)

    def greet_lines(d):
        greet(row, ((z + d) % Z) * C + k)
        greet(((y + d) % Y) * X + x, col)
        greet(((y + d) % Y) * X + x, other)

    def greet_x(d):
        greet(y * X + (x + d) % X, col)
        greet(y * X + (x + d) % X, other)

    loop(Z, greet_lines, 1)
    loop(X, greet_x, 1)
    greet(row, other)

    @pl.when(y != z)
    def _():
        def greet_cross(d):
            greet(((y + d) % Y) * X + x, y * C + k)

            @pl.when((z + d) % Z != y)
            def _():
                greet(z * X + x, ((z + d) % Z) * C + k)

        loop(Z, greet_cross, 1)

    loads[0].wait()
    loads[1].wait()
    labels = lax.broadcasted_iota(jnp.int32, (NCOL, BS), 0)
    em = emis[...]

    def emit(step):
        onehot = (labels == tok[step : step + 1, :]).astype(F32)
        out = lax.dot_general(
            onehot, em, (((0,), (0,)), ((), ())), precision=lax.Precision.HIGHEST, preferred_element_type=F32
        )
        return out.reshape(G, T, RB)

    loads[2].wait()
    tsend[0] = emit(0) * beta0[...]
    tsend[1] = emit(1)

    apart = ((y - z + Z) % Z + Z - 1) // Z
    pl.semaphore_wait(bar, 3 * (Z - 1) + 2 * (X - 1) + 1 + apart * (2 * Z - 3))

    def transpose(src, dst, i):
        @pl.when(y != z)
        def _():
            remote(src, dst, t_s.at[i], t_r.at[i], z * X + x, y * C + k).start()

        @pl.when(y == z)
        def _():
            pltpu.make_async_copy(src, dst, t_r.at[i]).start()

    for g in range(G):
        transpose(tsend.at[0, g], tw.at[0, g], g)

    def alpha_step(i):
        if i < 4:
            b = (z - i + Z) % Z
            ref = al.at[:, :, b, k]
            if i:
                wait(ref, a_r.at[b])
            remote(ref, ref, a_s.at[i], a_r.at[b], row, ((z + 1) % Z) * C + k).start()
        if i < 3:
            b = (z + i) % Z
            ref = al.at[:, :, b, k]
            if i:
                wait(ref, a_r.at[b])
            remote(ref, ref, a_s.at[4 + i], a_r.at[b], row, ((z + Z - 1) % Z) * C + k).start()
        if i == 4:
            for b in ((z + 4) % Z, (z + 3) % Z):
                wait(al.at[:, :, b, k], a_r.at[b])
            half = al.at[:, :, :, k]
            remote(half, half, ap.at[0], ap.at[1], row, other).start()

    def y_sends(step, g, src):
        dst = w.at[step, slot, g, y, k]
        recv = y_r.at[step, g, y]

        @pl.when(k == kd)
        def _():
            pltpu.make_async_copy(src, dst, recv).start()

        @pl.when(k != kd)
        def _():
            remote(src, dst, y_s.at[step, g, 1], recv, row, other).start()

        def send(j):
            to = (y + near_first(j)) % Y
            remote(src, dst, y_s.at[step, g, 0], recv, to * X + x, z * C + kd).start()

        loop(Y, send, 1)

    def x_sends(step, g):
        @pl.when(k == kd)
        def _():
            def send(j):
                s = (y + near_first(j)) % Y
                ref = w.at[step, slot, g, s]
                wait(ref, y_r.at[step, g, s])
                for d, to in enumerate((xp, xm)):
                    theirs = ((q + 1 + 2 * d) % 4) // 2
                    on = 1 - (j + theirs) % 2
                    i = on * (j // 2) + (1 - on) * 4
                    remote(ref, ref, x_s.at[step, g, d], x_r.at[step, g, i], y * X + to, col).start()

            loop(Y, send)

    def forwards(step, g):
        def send(i):
            s = (y + near_first(2 * i + fhalf)) % Y
            ref = w.at[step, fslot, g, s]
            wait(ref, x_r.at[step, g, i])
            remote(ref, ref, f_s.at[step, g], x_r.at[step, g, 5], y * X + fx, col).start()

        loop(Y // 2, send)

    def arrivals(step, g):
        wait(w.at[step, fslot, g, pl.ds(0, Y // 2)], x_r.at[step, g, 4])

        @pl.when(k != kd)
        def _():
            wait(w.at[step, slot, g], x_r.at[step, g, 5])

    def product(step, g):
        acc = None
        for sl in range(2):
            hi, lo = split(w[step, sl, g].reshape(HALF, RB))
            cols = slice(sl * RB, (sl + 1) * RB)
            both = dot(jnp.concatenate([hi, lo], axis=0), t_hi[:, cols], NT)
            part = both[:HALF] + both[HALF:] + dot(hi, t_lo[:, cols], NT)
            acc = part if acc is None else acc + part
        ub[step, g] = acc.reshape(Z, C, T, RB)
        remote(ub.at[step, g, :, 1 - k], pr.at[step, g], p_s.at[step, g], p_r.at[step, g], row, other).start()

    def sums_out(step, g):
        wait(pr.at[step, g], p_r.at[step, g])
        u = ub[step, g, :, k] + pr[step, g]
        ub[step, g, :, k] = u
        dst = cr.at[step, g, z]
        recv = c_r.at[step, g]

        def send(j):
            if step == 0:
                s = (y + near_first(j)) % Y
                r, c = s * X + x, y * C + k
            else:
                s = (z + near_first(j)) % Z
                r, c = row, s * C + k
            remote(ub.at[step, g, s, k], dst, c_s.at[step, g, 0], recv, r, c).start()

        loop(Z, send, 1)
        if step == 0:
            src = ub.at[step, g, y, k]

            @pl.when(y != z)
            def _():
                remote(src, dst, c_s.at[step, g, 1], recv, row, y * C + k).start()

            @pl.when(y == z)
            def _():
                pltpu.make_async_copy(src, dst, recv).start()
        else:
            pltpu.make_async_copy(ub.at[step, g, z, k], dst, recv).start()

    def reduced(step, g):
        wait(cr.at[step, g], c_r.at[step, g])
        acc = cr[step, g, 0]
        for i in range(1, Z):
            acc = acc + cr[step, g, i]
        return acc

    def next_weighted(g):
        wblk[g] = reduced(0, g) * tw[1, g]
        y_sends(1, g, wblk.at[g])

    def z_part(step, g):
        prod = (ub[step, g, :, k] * al[step, g, :, k]).reshape(HALF // C, RB)
        part = prod[:, 0:128]
        for i in range(1, RB // 128):
            part = part + prod[:, i * 128 : (i + 1) * 128]
        zpart[step, g] = part

    def z_sum(parts):
        v = parts[0]
        for p in parts[1:]:
            v = v + p
        return v

    def z_first(step):
        part = zpart[step].reshape(SEQ // C, 128)
        zz[step, z] = jnp.broadcast_to(jnp.sum(jnp.transpose(part), axis=0, keepdims=True), (8, SEQ // C))

        def send(d):
            ref = zz.at[step, z]
            remote(ref, ref, z_s.at[step, 0], z_r.at[step, 0], row, ((z + d) % Z) * C + k).start()

        loop(Z, send, 1)

    def z_second(step):
        wait(zz.at[step, pl.ds(0, Z - 1)], z_r.at[step, 0])
        zy[step, y] = z_sum([zz[step, i] for i in range(Z)])

        def send(d):
            ref = zy.at[step, y]
            remote(ref, ref, z_s.at[step, 1], z_r.at[step, 1], ((y + d) % Y) * X + x, col).start()

        loop(Y, send, 1)

    def z_third(step):
        wait(zy.at[step, pl.ds(0, Y - 1)], z_r.at[step, 1])
        zx[step, x * C + k] = z_sum([zy[step, i] for i in range(Y)])
        ref = zx.at[step, x * C + k]

        def send(d):
            remote(ref, ref, z_s.at[step, 2], z_r.at[step, 2], y * X + (x + d) % X, col).start()
            remote(ref, ref, z_s.at[step, 2], z_r.at[step, 2], y * X + (x + d) % X, other).start()

        loop(X, send, 1)
        remote(ref, ref, z_s.at[step, 2], z_r.at[step, 2], row, other).start()

    def z_last(step):
        wait(zx.at[step, pl.ds(0, X * C - 1)], z_r.at[step, 2])
        for c in range(C):
            v = z_sum([zx[step, i * C + c, 0:1, :] for i in range(X)])
            zc[step, :, :, c] = jnp.transpose(jnp.broadcast_to(v, (128, SEQ // C))).reshape(G, Z, T, 128)

    def scaled_columns(step, sl):
        inv = 1.0 / zc[step].reshape(SEQ, 128)
        return split(w[step, sl].reshape(SEQ, RB) * jnp.concatenate([inv] * (RB // 128), axis=1))

    def counts_part(step, sl):
        hi, lo = scaled_columns(step, sl)
        return dot(at_hi[step], hi, NN) + dot(at_lo[step], hi, NN) + dot(at_hi[step], lo, NN)

    def alphas_turned():
        wait(al.at[:, :, :, 1 - k], ap.at[1])
        for step in range(STEPS):
            v = al[step].reshape(SEQ, RB)
            for i in range(RB // 128):
                hi, lo = split(jnp.transpose(v[:, i * 128 : (i + 1) * 128]))
                at_hi[step, i * 128 : (i + 1) * 128, :] = hi
                at_lo[step, i * 128 : (i + 1) * 128, :] = lo

    loads[4].wait()

    def split_rows(i):
        r = pl.ds(pl.multiple_of(i * 64, 64), 64)
        hi, lo = split(t_f[r, :])
        t_hi[r, :] = hi
        t_lo[r, :] = lo

    loop(RB // 64, split_rows)

    for g in range(G):
        wait(tw.at[0, g], t_r.at[g])
        y_sends(0, g, tw.at[0, g])
    transpose(tsend.at[1], tw.at[1], 2)
    loads[3].wait()
    alpha_step(0)
    x_sends(0, 0)
    forwards(0, 0)
    x_sends(0, 1)
    alpha_step(1)
    arrivals(0, 0)
    product(0, 0)
    forwards(0, 1)
    sums_out(0, 0)
    alpha_step(2)
    arrivals(0, 1)
    product(0, 1)
    alpha_step(3)
    sums_out(0, 1)

    wait(tw.at[1], t_r.at[2])
    next_weighted(0)
    alpha_step(4)
    z_part(0, 0)
    z_part(0, 1)
    x_sends(1, 0)
    next_weighted(1)
    forwards(1, 0)
    z_first(0)
    x_sends(1, 1)
    alphas_turned()
    arrivals(1, 0)
    product(1, 0)
    forwards(1, 1)
    sums_out(1, 0)
    z_second(0)
    z_part(1, 0)
    arrivals(1, 1)
    product(1, 1)
    sums_out(1, 1)
    z_part(1, 1)
    z_first(1)

    z_third(0)
    z_last(0)
    z_second(1)
    counts_out[:, :RB] = counts_part(0, 0)
    z_third(1)
    counts_out[:, RB:] = counts_part(0, 1)

    @pl.when(y != z)
    def _():
        wait(tsend.at[0, 0], t_s.at[0])
        wait(tsend.at[0, 1], t_s.at[1])
        wait(tsend.at[1], t_s.at[2])
        for g in range(G):
            wait(wblk.at[g], c_s.at[0, g, 1])

    for step in range(STEPS):
        for g in range(G):
            wait(cr.at[step, g, pl.ds(0, Y - 1)], y_s.at[step, g, 0])
            wait(cr.at[step, g, pl.ds(0, Z - 1)], c_s.at[step, g, 0])
            wait(pr.at[step, g], p_s.at[step, g])
            wait(w.at[step, 0, g, pl.ds(0, Y // 2)], f_s.at[step, g])

            @pl.when(k != kd)
            def _():
                wait(wblk.at[g], y_s.at[step, g, 1])

            @pl.when(k == kd)
            def _():
                wait(w.at[step, 0, g], x_s.at[step, g, 0])
                wait(w.at[step, 0, g], x_s.at[step, g, 1])

        for i in range(3):
            wait(zz.at[step, pl.ds(0, 7)], z_s.at[step, i])
    for i in range(7):
        wait(al.at[:, :, 0, 0], a_s.at[i])
    wait(al.at[:, :, :, 0], ap.at[0])

    z_last(1)
    for sl in range(2):
        cols = slice(sl * RB, (sl + 1) * RB)
        counts_out[:, cols] = (t_f[:, cols] * (counts_out[:, cols] + counts_part(1, sl))) * FACTOR
    for g in range(G):
        norm = zc[1, g, z, k]
        beta_out[g] = (reduced(1, g) / jnp.concatenate([norm] * (RB // 128), axis=1)) * float(H)


def per_device(transition, alphas, beta_last, emission, token_ids):
    hbm = pl.BlockSpec(memory_space=pltpu.HBM)
    vmem = pl.BlockSpec(memory_space=pltpu.VMEM)
    dma = pltpu.SemaphoreType.DMA
    beta, counts = pl.pallas_call(
        kernel,
        out_shape=(
            jax.ShapeDtypeStruct((G, T, RB), F32),
            jax.ShapeDtypeStruct((RB, CB), F32),
        ),
        in_specs=[hbm] * 5,
        out_specs=(vmem, vmem),
        scratch_shapes=[
            pltpu.VMEM((RB, CB), F32),
            pltpu.VMEM((RB, CB), BF16),
            pltpu.VMEM((RB, CB), BF16),
            pltpu.VMEM((NCOL, RB), F32),
            pltpu.VMEM((G, T, RB), F32),
            pltpu.VMEM((STEPS, BS), jnp.int32),
            pltpu.VMEM((STEPS, G, Z, C, T, RB), F32),
            pltpu.VMEM((STEPS, RB, SEQ), BF16),
            pltpu.VMEM((STEPS, RB, SEQ), BF16),
            pltpu.VMEM((2, G, T, RB), F32),
            pltpu.VMEM((2, G, T, RB), F32),
            pltpu.VMEM((G, T, RB), F32),
            pltpu.VMEM((STEPS, 2, G, Z, C, T, RB), F32),
            pltpu.VMEM((STEPS, G, Z, C, T, RB), F32),
            pltpu.VMEM((STEPS, G, Z, T, RB), F32),
            pltpu.VMEM((STEPS, G, Z, T, RB), F32),
            pltpu.VMEM((STEPS, G, HALF // C, 128), F32),
            pltpu.VMEM((STEPS, Z, 8, 128), F32),
            pltpu.VMEM((STEPS, Y, 8, 128), F32),
            pltpu.VMEM((STEPS, X * C, 8, 128), F32),
            pltpu.VMEM((STEPS, G, Z, C, T, 128), F32),
            dma((5,)),
            dma((3,)), dma((3,)),
            dma((7,)), dma((Z,)),
            dma((2,)),
            dma((STEPS, G, 2)), dma((STEPS, G, Y)),
            dma((STEPS, G, 2)), dma((STEPS, G, 6)),
            dma((STEPS, G)),
            dma((STEPS, G)), dma((STEPS, G)),
            dma((STEPS, G, 2)), dma((STEPS, G)),
            dma((STEPS, 3)), dma((STEPS, 3)),
        ],
        compiler_params=pltpu.CompilerParams(
            collective_id=0, has_side_effects=True, vmem_limit_bytes=60 * 1024 * 1024
        ),
    )(
        transition,
        alphas.reshape(STEPS, G, T, RB),
        beta_last.reshape(G, T, RB),
        emission,
        token_ids,
    )
    return beta.reshape(BS, RB), counts


def solution(mesh):
    return jax.shard_map(
        per_device,
        mesh=mesh,
        in_specs=(
            P("row", "col"),
            P(None, "col", "row"),
            P("col", "row"),
            P(None, "row"),
            P(None, "col"),
        ),
        out_specs=(P("col", "row"), P("row", "col")),
        check_vma=False,
    )
```

```python
import jax
import jax.numpy as jnp
from jax import lax
from jax.experimental import pallas as pl
from jax.experimental.pallas import tpu as pltpu
from jax.sharding import PartitionSpec as P

H = 16384
STEPS = 2
SEQ = 256
X, Y, Z, C = 4, 8, 8, 2
G = 2
BS = SEQ // (Z * C)
T = BS // G
HALF = SEQ // G
RB = H // (X * Y)
CB = H // (Z * C)
NCOL = 128
FACTOR = float(H * H) / float(SEQ * STEPS)
F32 = jnp.float32
BF16 = jnp.bfloat16
MESH = pl.DeviceIdType.MESH
NT = ((1,), (1,))
NN = ((1,), (0,))


def loop(n, body, start=0):
    def step(i, carry):
        body(i)
        return carry

    lax.fori_loop(start, n, step, 0)


def remote(src, dst, send, recv, row, col):
    return pltpu.make_async_remote_copy(
        src_ref=src, dst_ref=dst, send_sem=send, recv_sem=recv, device_id=(row, col), device_id_type=MESH
    )


def wait(ref, sem):
    pltpu.make_async_copy(ref, ref, sem).wait()


def near_first(j):
    return (j % 2) * ((j + 1) // 2) + (1 - j % 2) * (8 - j // 2)


def split(v):
    hi = v.astype(BF16)
    return hi, (v - hi.astype(F32)).astype(BF16)


def dot(a, b, dims):
    return lax.dot_general(a, b, (dims, ((), ())), preferred_element_type=F32)


def kernel(
    trans_hbm, alphas_hbm, beta_hbm, emis_hbm, tok_hbm,
    beta_out, counts_out,
    t_f, t_hi, t_lo, emis, beta0, tok, al, at_hi, at_lo, tsend, wblk, w, ub, pr, cr, g1, zpart, zs, zz, zz1, zy, zx, zc,
    ld, a_s, a_r, ap, y_s, y_r, x_s, x_r, p_s, p_r, c_s, c_r, z_s, z_r,
):
    row = lax.axis_index("row")
    col = lax.axis_index("col")
    x, y, z, k = row % X, row // X, col // C, col % C
    kd = x // 2
    slot = x % 2
    fslot = 1 - slot
    other = z * C + 1 - k

    loads = [
        pltpu.make_async_copy(tok_hbm, tok, ld.at[0]),
        pltpu.make_async_copy(emis_hbm, emis, ld.at[1]),
        pltpu.make_async_copy(beta_hbm, beta0, ld.at[2]),
        pltpu.make_async_copy(alphas_hbm, al.at[:, :, z, k], ld.at[3]),
        pltpu.make_async_copy(trans_hbm, t_f, ld.at[4]),
    ]
    for c in loads:
        c.start()

    bar = pltpu.get_barrier_semaphore()

    def greet(r, c):
        pl.semaphore_signal(bar, inc=1, device_id=(r, c), device_id_type=MESH)

    owner = 1 - (k + kd) % 2
    diag = 1 - ((y - z + Z) % Z + Z - 1) // Z

    def greet_lines(d):
        greet(row, ((z + d) % Z) * C)
        greet(row, ((z + d) % Z) * C + 1)
        greet(((y + d) % Y) * X + x, col)
        greet(((y + d) % Y) * X + x, y * C + kd)

    def greet_x(d):
        greet(y * X + (x + d) % X, col)
        greet(y * X + (x + d) % X, other)

    loop(Z, greet_lines, 1)
    loop(X, greet_x, 1)
    greet(row, other)

    @pl.when(owner * diag == 0)
    def _():
        greet(row, y * C + kd)

    @pl.when(owner == 1)
    def _():
        def greet_back(d):
            greet(z * X + x, ((z + d) % Z) * C + 1 - k)

            @pl.when(diag * (Z - d) != Z)
            def _():
                greet(z * X + x, ((z + d) % Z) * C + k)

        loop(Z, greet_back)

    loads[0].wait()
    loads[1].wait()
    labels = lax.broadcasted_iota(jnp.int32, (NCOL, BS), 0)
    em = emis[...]

    def emit(step):
        onehot = (labels == tok[step : step + 1, :]).astype(F32)
        out = lax.dot_general(
            onehot, em, (((0,), (0,)), ((), ())), precision=lax.Precision.HIGHEST, preferred_element_type=F32
        )
        return out.reshape(G, T, RB)

    loads[2].wait()
    tsend[0] = emit(0) * beta0[...]
    tsend[1] = emit(1)

    pl.semaphore_wait(bar, 3 * (Z - 1) + 2 * (X - 1) + 1 + Y + owner * (Z * C - 2 * diag))

    def alpha_step(i):
        if i < 4:
            b = (z - i + Z) % Z
            ref = al.at[:, :, b, k]
            if i:
                wait(ref, a_r.at[b])
            remote(ref, ref, a_s.at[i], a_r.at[b], row, ((z + 1) % Z) * C + k).start()
        if i < 3:
            b = (z + i) % Z
            ref = al.at[:, :, b, k]
            if i:
                wait(ref, a_r.at[b])
            remote(ref, ref, a_s.at[4 + i], a_r.at[b], row, ((z + Z - 1) % Z) * C + k).start()
        if i == 4:
            for b in ((z + 4) % Z, (z + 3) % Z):
                wait(al.at[:, :, b, k], a_r.at[b])
            half = al.at[:, :, :, k]
            remote(half, half, ap.at[0], ap.at[1], row, other).start()

    def y_sends(step, g, src):
        dst = w.at[step, slot, g, z, k]
        recv = y_r.at[step, g, z]

        @pl.when(owner * diag == 1)
        def _():
            pltpu.make_async_copy(src, dst, recv).start()

        @pl.when(owner * diag == 0)
        def _():
            remote(src, dst, y_s.at[step, g, 1], recv, row, y * C + kd).start()

        def send(j):
            to = (y + near_first(j)) % Y
            remote(src, dst, y_s.at[step, g, 0], recv, to * X + x, y * C + kd).start()

        loop(Y, send, 1)

    def x_sends(step, g):
        @pl.when(owner == 1)
        def _():
            def send(j):
                s = (z + near_first(j)) % Z
                ref = w.at[step, slot, g, s]
                wait(ref, y_r.at[step, g, s])
                for d in (2, 1, 3):
                    remote(ref, ref, x_s.at[step, g], x_r.at[step, g], y * X + (x + d) % X, col).start()

            loop(Z, send)

    def arrivals(step, g):
        @pl.when(owner == 1)
        def _():
            wait(w.at[step, fslot, g], x_r.at[step, g])

        @pl.when(owner == 0)
        def _():
            wait(w.at[step, :, g], x_r.at[step, g])

    def product(step, g):
        acc = None
        for sl in range(2):
            hi, lo = split(w[step, sl, g].reshape(HALF, RB))
            cols = slice(sl * RB, (sl + 1) * RB)
            both = dot(jnp.concatenate([hi, lo], axis=0), t_hi[:, cols], NT)
            part = both[:HALF] + both[HALF:] + dot(hi, t_lo[:, cols], NT)
            acc = part if acc is None else acc + part
        ub[step, g] = acc.reshape(Z, C, T, RB)
        remote(ub.at[step, g, :, 1 - k], pr.at[step, g], p_s.at[step, g], p_r.at[step, g], row, other).start()

    def sums_out(step, g):
        wait(pr.at[step, g], p_r.at[step, g])
        u = ub[step, g, :, k] + pr[step, g]
        ub[step, g, :, k] = u
        dst = cr.at[step, g, z]
        recv = c_r.at[step, g]

        def send(j):
            s = (z + near_first(j)) % Z
            remote(ub.at[step, g, s, k], dst, c_s.at[step, g], recv, row, s * C + k).start()

        loop(Z, send, 1)
        pltpu.make_async_copy(ub.at[step, g, z, k], dst, recv).start()

    def reduced(step, g):
        wait(cr.at[step, g], c_r.at[step, g])
        acc = cr[step, g, 0]
        for i in range(1, Z):
            acc = acc + cr[step, g, i]
        return acc

    def next_weighted(g):
        wblk[g] = reduced(0, g) * tsend[1, g]
        y_sends(1, g, wblk.at[g])

    def lanes(parts):
        acc = None
        for v in parts:
            for i in range(RB // 128):
                t = v[:, i * 128 : (i + 1) * 128]
                acc = t if acc is None else acc + t
        return acc

    def z_part_0():
        v = (ub[0, :, :, k] * al[0, :, :, k]).reshape(SEQ // C, RB)
        zz[0, z] = z_row(lanes([v]))

    def z_row(part):
        return jnp.broadcast_to(jnp.sum(jnp.transpose(part), axis=0, keepdims=True), (8, SEQ // C))

    def z_first_0():
        def send(d):
            ref = zz.at[0, z]
            remote(ref, ref, z_s.at[0, 0], z_r.at[0, 0], row, ((z + d) % Z) * C + k).start()

        loop(Z, send, 1)

    def alpha_transition():
        a_hi, a_lo = split(al[1].reshape(SEQ, RB))
        for sl in range(2):
            cols = slice(sl * RB, (sl + 1) * RB)
            g1[sl] = (
                dot(a_hi, t_hi[:, cols], NN) + dot(a_lo, t_hi[:, cols], NN) + dot(a_hi, t_lo[:, cols], NN)
            ).reshape(G, Z, C, T, RB)

    def z_part_1(g):
        zpart[g] = lanes([(g1[sl, g] * w[1, sl, g]).reshape(HALF, RB) for sl in range(2)]).reshape(Z, C, T, 128)

    def z_first_1():
        for c in range(C):
            zs[c] = z_row(zpart[:, :, c].reshape(SEQ // C, 128))
        zz1[z * C + k] = zs[k]

        def send(d):
            for c in range(C):
                remote(zs.at[c], zz1.at[z * C + k], z_s.at[1, 0], z_r.at[1, 0], row, ((z + d) % Z) * C + c).start()

        loop(Z, send, 1)
        remote(zs.at[1 - k], zz1.at[z * C + k], z_s.at[1, 0], z_r.at[1, 0], row, other).start()

    def z_sum(parts):
        v = parts[0]
        for p in parts[1:]:
            v = v + p
        return v

    def z_second(step):
        if step == 0:
            wait(zz.at[0, pl.ds(0, Z - 1)], z_r.at[0, 0])
            zy[step, y] = z_sum([zz[0, i] for i in range(Z)])
        else:
            wait(zz1.at[pl.ds(0, Z * C - 1)], z_r.at[1, 0])
            zy[step, y] = z_sum([zz1[i] for i in range(Z * C)])

        def send(d):
            ref = zy.at[step, y]
            remote(ref, ref, z_s.at[step, 1], z_r.at[step, 1], ((y + d) % Y) * X + x, col).start()

        loop(Y, send, 1)

    def z_third(step):
        wait(zy.at[step, pl.ds(0, Y - 1)], z_r.at[step, 1])
        zx[step, x * C + k] = z_sum([zy[step, i] for i in range(Y)])
        ref = zx.at[step, x * C + k]

        def send(d):
            remote(ref, ref, z_s.at[step, 2], z_r.at[step, 2], y * X + (x + d) % X, col).start()
            remote(ref, ref, z_s.at[step, 2], z_r.at[step, 2], y * X + (x + d) % X, other).start()

        loop(X, send, 1)
        remote(ref, ref, z_s.at[step, 2], z_r.at[step, 2], row, other).start()

    def z_last(step):
        wait(zx.at[step, pl.ds(0, X * C - 1)], z_r.at[step, 2])
        for c in range(C):
            v = z_sum([zx[step, i * C + c, 0:1, :] for i in range(X)])
            zc[step, :, :, c] = jnp.transpose(jnp.broadcast_to(v, (128, SEQ // C))).reshape(G, Z, T, 128)

    def scaled_columns(step, sl):
        inv = 1.0 / zc[step].reshape(SEQ, 128)
        return split(w[step, sl].reshape(SEQ, RB) * jnp.concatenate([inv] * (RB // 128), axis=1))

    def counts_part(step, sl):
        hi, lo = scaled_columns(step, sl)
        return dot(at_hi[step], hi, NN) + dot(at_lo[step], hi, NN) + dot(at_hi[step], lo, NN)

    def alphas_turned():
        wait(al.at[:, :, :, 1 - k], ap.at[1])
        for step in range(STEPS):
            v = al[step].reshape(SEQ, RB)
            for i in range(RB // 128):
                hi, lo = split(jnp.transpose(v[:, i * 128 : (i + 1) * 128]))
                at_hi[step, i * 128 : (i + 1) * 128, :] = hi
                at_lo[step, i * 128 : (i + 1) * 128, :] = lo

    for g in range(G):
        y_sends(0, g, tsend.at[0, g])
    loads[3].wait()
    alpha_step(0)

    loads[4].wait()

    def split_rows(i):
        r = pl.ds(pl.multiple_of(i * 64, 64), 64)
        hi, lo = split(t_f[r, :])
        t_hi[r, :] = hi
        t_lo[r, :] = lo

    loop(RB // 64, split_rows)

    x_sends(0, 0)
    x_sends(0, 1)
    alpha_step(1)
    arrivals(0, 0)
    product(0, 0)
    sums_out(0, 0)
    alpha_step(2)
    arrivals(0, 1)
    product(0, 1)
    alpha_step(3)
    sums_out(0, 1)

    next_weighted(0)
    alpha_step(4)
    z_part_0()
    z_first_0()
    x_sends(1, 0)
    next_weighted(1)
    x_sends(1, 1)
    alphas_turned()
    alpha_transition()
    z_second(0)
    arrivals(1, 0)
    product(1, 0)
    z_part_1(0)
    sums_out(1, 0)
    z_third(0)
    arrivals(1, 1)
    z_part_1(1)
    z_first_1()
    product(1, 1)
    z_last(0)
    sums_out(1, 1)

    counts_out[:, :RB] = counts_part(0, 0)
    z_second(1)
    counts_out[:, RB:] = counts_part(0, 1)
    z_third(1)

    for step in range(STEPS):
        for g in range(G):
            wait(cr.at[step, g, pl.ds(0, Y - 1)], y_s.at[step, g, 0])
            wait(cr.at[step, g, pl.ds(0, Z - 1)], c_s.at[step, g])
            wait(pr.at[step, g], p_s.at[step, g])

            @pl.when(owner * diag == 0)
            def _():
                wait(wblk.at[g], y_s.at[step, g, 1])

            @pl.when(owner == 1)
            def _():
                for i in range(X - 1):
                    wait(w.at[step, 0, g], x_s.at[step, g])

        wait(zz1.at[pl.ds(0, (Z - 1, Z * C - 1)[step])], z_s.at[step, 0])
        wait(zy.at[0, pl.ds(0, Y - 1)], z_s.at[step, 1])
        wait(zx.at[0, pl.ds(0, X * C - 1)], z_s.at[step, 2])
    for i in range(7):
        wait(al.at[:, :, 0, 0], a_s.at[i])
    wait(al.at[:, :, :, 0], ap.at[0])

    z_last(1)
    for sl in range(2):
        cols = slice(sl * RB, (sl + 1) * RB)
        counts_out[:, cols] = (t_f[:, cols] * (counts_out[:, cols] + counts_part(1, sl))) * FACTOR
    for g in range(G):
        norm = zc[1, g, z, k]
        beta_out[g] = (reduced(1, g) / jnp.concatenate([norm] * (RB // 128), axis=1)) * float(H)


def per_device(transition, alphas, beta_last, emission, token_ids):
    hbm = pl.BlockSpec(memory_space=pltpu.HBM)
    vmem = pl.BlockSpec(memory_space=pltpu.VMEM)
    dma = pltpu.SemaphoreType.DMA
    beta, counts = pl.pallas_call(
        kernel,
        out_shape=(
            pltpu.VMEM((G, T, RB), F32),
            pltpu.VMEM((RB, CB), F32),
        ),
        in_specs=[hbm] * 5,
        out_specs=(vmem, vmem),
        scratch_shapes=[
            pltpu.VMEM((RB, CB), F32),
            pltpu.VMEM((RB, CB), BF16),
            pltpu.VMEM((RB, CB), BF16),
            pltpu.VMEM((NCOL, RB), F32),
            pltpu.VMEM((G, T, RB), F32),
            pltpu.VMEM((STEPS, BS), jnp.int32),
            pltpu.VMEM((STEPS, G, Z, C, T, RB), F32),
            pltpu.VMEM((STEPS, RB, SEQ), BF16),
            pltpu.VMEM((STEPS, RB, SEQ), BF16),
            pltpu.VMEM((2, G, T, RB), F32),
            pltpu.VMEM((G, T, RB), F32),
            pltpu.VMEM((STEPS, 2, G, Z, C, T, RB), F32),
            pltpu.VMEM((STEPS, G, Z, C, T, RB), F32),
            pltpu.VMEM((STEPS, G, Z, T, RB), F32),
            pltpu.VMEM((STEPS, G, Z, T, RB), F32),
            pltpu.VMEM((2, G, Z, C, T, RB), F32),
            pltpu.VMEM((G, Z, C, T, 128), F32),
            pltpu.VMEM((C, 8, 128), F32),
            pltpu.VMEM((1, Z, 8, 128), F32),
            pltpu.VMEM((Z * C, 8, 128), F32),
            pltpu.VMEM((STEPS, Y, 8, 128), F32),
            pltpu.VMEM((STEPS, X * C, 8, 128), F32),
            pltpu.VMEM((STEPS, G, Z, C, T, 128), F32),
            dma((5,)),
            dma((7,)), dma((Z,)),
            dma((2,)),
            dma((STEPS, G, 2)), dma((STEPS, G, Y)),
            dma((STEPS, G)), dma((STEPS, G)),
            dma((STEPS, G)), dma((STEPS, G)),
            dma((STEPS, G)), dma((STEPS, G)),
            dma((STEPS, 3)), dma((STEPS, 3)),
        ],
        compiler_params=pltpu.CompilerParams(
            collective_id=0, has_side_effects=True, vmem_limit_bytes=52 * 1024 * 1024
        ),
    )(
        transition,
        alphas.reshape(STEPS, G, T, RB),
        beta_last.reshape(G, T, RB),
        emission,
        token_ids,
    )
    return beta.reshape(BS, RB), counts


def solution(mesh):
    return jax.shard_map(
        per_device,
        mesh=mesh,
        in_specs=(
            P("row", "col"),
            P(None, "col", "row"),
            P("col", "row"),
            P(None, "row"),
            P(None, "col"),
        ),
        out_specs=(P("col", "row"), P("row", "col")),
        check_vma=False,
    )
```

```python
import jax
import jax.numpy as jnp
from jax import lax
from jax.experimental import pallas as pl
from jax.experimental.pallas import tpu as pltpu
from jax.sharding import PartitionSpec as P

H = 16384
STEPS = 2
SEQ = 256
X, Y, Z, C = 4, 8, 8, 2
G = 2
BS = SEQ // (Z * C)
T = BS // G
HALF = SEQ // G
RB = H // (X * Y)
CB = H // (Z * C)
NCOL = 128
FACTOR = float(H * H) / float(SEQ * STEPS)
F32 = jnp.float32
BF16 = jnp.bfloat16
MESH = pl.DeviceIdType.MESH
NT = ((1,), (1,))
NN = ((1,), (0,))


def loop(n, body, start=0):
    def step(i, carry):
        body(i)
        return carry

    lax.fori_loop(start, n, step, 0)


def remote(src, dst, send, recv, row, col):
    return pltpu.make_async_remote_copy(
        src_ref=src, dst_ref=dst, send_sem=send, recv_sem=recv, device_id=(row, col), device_id_type=MESH
    )


def wait(ref, sem):
    pltpu.make_async_copy(ref, ref, sem).wait()


def near_first(j):
    return (j % 2) * ((j + 1) // 2) + (1 - j % 2) * (8 - j // 2)


def split(v):
    hi = v.astype(BF16)
    return hi, (v - hi.astype(F32)).astype(BF16)


def dot(a, b, dims):
    return lax.dot_general(a, b, (dims, ((), ())), preferred_element_type=F32)


def kernel(
    trans_hbm, alphas_hbm, beta_hbm, emis_hbm, tok_hbm,
    beta_out, counts_out,
    t_f, t_hi, t_lo, emis, beta0, tok, al, at, at_hi, at_lo, tsend, wblk, w, w_hi, w_lo, ub, pr, cr, g1, gx, zpart, zz, zz1, zy, zy1, zx, zx1, zc,
    ld, a_s, a_r, ap, b_s, b_r, g_s, g_r, y_s, y_r, x_s, x_r, p_s, p_r, c_s, c_r, z_s, z_r,
):
    row = lax.axis_index("row")
    col = lax.axis_index("col")
    x, y, z, k = row % X, row // X, col // C, col % C
    kd = x // 2
    slot = x % 2
    fslot = 1 - slot
    other = z * C + 1 - k

    loads = [
        pltpu.make_async_copy(tok_hbm, tok, ld.at[0]),
        pltpu.make_async_copy(emis_hbm, emis, ld.at[1]),
        pltpu.make_async_copy(beta_hbm, beta0, ld.at[2]),
        pltpu.make_async_copy(alphas_hbm, al.at[:, :, k, z], ld.at[3]),
        pltpu.make_async_copy(trans_hbm, t_f, ld.at[4]),
    ]
    for c in loads:
        c.start()

    bar = pltpu.get_barrier_semaphore()

    def greet(r, c):
        pl.semaphore_signal(bar, inc=1, device_id=(r, c), device_id_type=MESH)

    owner = 1 - (k + kd) % 2
    diag = 1 - ((y - z + Z) % Z + Z - 1) // Z

    def greet_lines(d):
        greet(row, ((z + d) % Z) * C)
        greet(row, ((z + d) % Z) * C + 1)
        greet(((y + d) % Y) * X + x, col)
        greet(((y + d) % Y) * X + x, y * C + kd)

    def greet_x(d):
        greet(y * X + (x + d) % X, col)
        greet(y * X + (x + d) % X, other)

    loop(Z, greet_lines, 1)
    loop(X, greet_x, 1)
    greet(row, other)

    @pl.when(owner * diag == 0)
    def _():
        greet(row, y * C + kd)

    @pl.when(owner == 1)
    def _():
        def greet_back(d):
            greet(z * X + x, ((z + d) % Z) * C + 1 - k)

            @pl.when(diag * (Z - d) != Z)
            def _():
                greet(z * X + x, ((z + d) % Z) * C + k)

        loop(Z, greet_back)

    loads[0].wait()
    loads[1].wait()
    labels = lax.broadcasted_iota(jnp.int32, (NCOL, BS), 0)
    em = emis[...]

    def emit(step):
        onehot = (labels == tok[step : step + 1, :]).astype(F32)
        out = lax.dot_general(
            onehot, em, (((0,), (0,)), ((), ())), precision=lax.Precision.HIGHEST, preferred_element_type=F32
        )
        return out.reshape(G, T, RB)

    loads[2].wait()
    tsend[0] = emit(0) * beta0[...]

    pl.semaphore_wait(bar, 3 * (Z - 1) + 2 * (X - 1) + 1 + Y + owner * (Z * C - 2 * diag))

    def alpha_1_sends():
        ref = al.at[1, :, k, z]

        def send(d):
            remote(ref, ref, b_s.at[0], b_r.at[0], row, ((z + d) % Z) * C + k).start()

        loop(Z, send, 1)

    def alpha_1_on():
        wait(al.at[1, :, k, pl.ds(0, Z - 1)], b_r.at[0])
        half = al.at[1, :, k]
        remote(half, half, b_s.at[1], b_r.at[1], row, other).start()

    def alpha_step(i):
        if i < 4:
            b = (z - i + Z) % Z
            ref = al.at[0, :, k, b]
            if i:
                wait(ref, a_r.at[b])
            remote(ref, ref, a_s.at[i], a_r.at[b], row, ((z + 1) % Z) * C + k).start()
        if i < 3:
            b = (z + i) % Z
            ref = al.at[0, :, k, b]
            if i:
                wait(ref, a_r.at[b])
            remote(ref, ref, a_s.at[4 + i], a_r.at[b], row, ((z + Z - 1) % Z) * C + k).start()
        if i == 4:
            for b in ((z + 4) % Z, (z + 3) % Z):
                wait(al.at[0, :, k, b], a_r.at[b])
            half = al.at[0, :, k]
            remote(half, half, ap.at[0], ap.at[1], row, other).start()

    def y_sends(step, g, src):
        dst = w.at[step, slot, g, z, k]
        recv = y_r.at[step, g, z]

        @pl.when(owner * diag == 1)
        def _():
            pltpu.make_async_copy(src, dst, recv).start()

        @pl.when(owner * diag == 0)
        def _():
            remote(src, dst, y_s.at[step, g, 1], recv, row, y * C + kd).start()

        def send(j):
            to = (y + near_first(j)) % Y
            remote(src, dst, y_s.at[step, g, 0], recv, to * X + x, y * C + kd).start()

        loop(Y, send, 1)

    def x_stage(step, g):
        @pl.when(owner == 1)
        def _():
            def send(j):
                s = (z + near_first(j)) % Z
                ref = w.at[step, slot, g, s]
                wait(ref, y_r.at[step, g, s])
                for d in (2, 1, 3):
                    remote(ref, ref, x_s.at[step, g], x_r.at[step, g], y * X + (x + d) % X, col).start()

            loop(Z, send)

    def arrivals(step, g):
        @pl.when(owner == 1)
        def _():
            wait(w.at[step, fslot, g], x_r.at[step, g])

        @pl.when(owner == 0)
        def _():
            wait(w.at[step, :, g], x_r.at[step, g])

    def product(step, g):
        acc = None
        for sl in range(2):
            hi, lo = split(jnp.concatenate([w[step, sl, g, :, c].reshape(HALF // C, RB) for c in range(C)], axis=0))
            w_hi[step, sl, g * HALF : (g + 1) * HALF, :] = hi
            w_lo[step, sl, g * HALF : (g + 1) * HALF, :] = lo
            cols = slice(sl * RB, (sl + 1) * RB)
            both = dot(jnp.concatenate([hi, lo], axis=0), t_hi[:, cols], NT)
            part = both[:HALF] + both[HALF:] + dot(hi, t_lo[:, cols], NT)
            acc = part if acc is None else acc + part
        ub[step, g] = acc.reshape(C, Z, T, RB)
        remote(ub.at[step, g, 1 - k], pr.at[step, g], p_s.at[step, g], p_r.at[step, g], row, other).start()

    def sums_out(step, g):
        wait(pr.at[step, g], p_r.at[step, g])
        ub[step, g, k] = ub[step, g, k] + pr[step, g]
        dst = cr.at[step, g, z]
        recv = c_r.at[step, g]

        def send(j):
            s = (z + near_first(j)) % Z
            remote(ub.at[step, g, k, s], dst, c_s.at[step, g], recv, row, s * C + k).start()

        loop(Z, send, 1)
        pltpu.make_async_copy(ub.at[step, g, k, z], dst, recv).start()

    def reduced(step, g):
        wait(cr.at[step, g], c_r.at[step, g])
        acc = cr[step, g, 0]
        for i in range(1, Z):
            acc = acc + cr[step, g, i]
        return acc

    def next_weighted(g):
        wblk[g] = reduced(0, g) * tsend[1, g]
        y_sends(1, g, wblk.at[g])

    def lanes(parts):
        acc = None
        for v in parts:
            for i in range(RB // 128):
                t = v[:, i * 128 : (i + 1) * 128]
                acc = t if acc is None else acc + t
        return acc

    def z_part_0():
        v = (ub[0, :, k] * al[0, :, k]).reshape(SEQ // C, RB)
        zz[0, z] = z_row(lanes([v]))

    def z_row(part):
        return jnp.broadcast_to(jnp.sum(jnp.transpose(part), axis=0, keepdims=True), (8, SEQ // C))

    def z_first_0():
        def send(d):
            ref = zz.at[0, z]
            remote(ref, ref, z_s.at[0, 0], z_r.at[0, 0], row, ((z + d) % Z) * C + k).start()

        loop(Z, send, 1)

    def alpha_transition():
        wait(al.at[1, :, 1 - k], b_r.at[1])
        a_hi, a_lo = split(al[1].reshape(SEQ, RB))
        for sl in range(2):
            cols = slice(sl * RB, (sl + 1) * RB)
            g1[sl] = dot(a_hi, t_hi[:, cols], NN) + dot(a_lo, t_hi[:, cols], NN) + dot(a_hi, t_lo[:, cols], NN)

        for d in (2, 1, 3, 0):
            to = (x + d) % X

            @pl.when(to // 2 == k)
            def _():
                if d:
                    remote(g1.at[to % 2], gx.at[x], g_s.at[d], g_r.at[0], y * X + to, col).start()
                else:
                    pltpu.make_async_copy(g1.at[to % 2], gx.at[x], g_r.at[0]).start()

    def alpha_transition_sum():
        @pl.when(owner == 1)
        def _():
            wait(gx, g_r.at[0])
            gx[0] = z_sum([gx[i] for i in range(X)])

    def z_part_1(g):
        @pl.when(owner == 1)
        def _():
            for c in range(C):
                a = g * HALF + c * (HALF // C)
                zpart[c, g] = lanes([gx[0, a : a + HALF // C, :] * w[1, slot, g, :, c].reshape(HALF // C, RB)])

    def z_first_1():
        @pl.when(owner == 1)
        def _():
            for c in range(C):
                zz1[z, c] = z_row(zpart[c].reshape(SEQ // C, 128))
            ref = zz1.at[z]

            def send(d):
                remote(ref, ref, z_s.at[1, 0], z_r.at[1, 0], row, ((z + d) % Z) * C + k).start()

            loop(Z, send, 1)

    def z_second_1():
        @pl.when(owner == 1)
        def _():
            wait(zz1.at[pl.ds(0, Z - 1)], z_r.at[1, 0])
            zy1[y] = z_sum([zz1[i] for i in range(Z)])
            ref = zy1.at[y]

            def send(d):
                remote(ref, ref, z_s.at[1, 1], z_r.at[1, 1], ((y + d) % Y) * X + x, col).start()

            loop(Y, send, 1)

    def z_third_1():
        @pl.when(owner == 1)
        def _():
            wait(zy1.at[pl.ds(0, Y - 1)], z_r.at[1, 1])
            zx1[x] = z_sum([zy1[i] for i in range(Y)])
            ref = zx1.at[x]

            def send(d):
                remote(ref, ref, z_s.at[1, 2], z_r.at[1, 2], y * X + (x + d) % X, col).start()
                remote(ref, ref, z_s.at[1, 2], z_r.at[1, 2], y * X + (x + d) % X, other).start()

            loop(X, send, 1)
            remote(ref, ref, z_s.at[1, 2], z_r.at[1, 2], row, other).start()

    def z_sum(parts):
        v = parts[0]
        for p in parts[1:]:
            v = v + p
        return v

    def z_second_0():
        wait(zz.at[0, pl.ds(0, Z - 1)], z_r.at[0, 0])
        zy[y] = z_sum([zz[0, i] for i in range(Z)])

        def send(d):
            ref = zy.at[y]
            remote(ref, ref, z_s.at[0, 1], z_r.at[0, 1], ((y + d) % Y) * X + x, col).start()

        loop(Y, send, 1)

    def z_third_0():
        wait(zy.at[pl.ds(0, Y - 1)], z_r.at[0, 1])
        zx[x * C + k] = z_sum([zy[i] for i in range(Y)])
        ref = zx.at[x * C + k]

        def send(d):
            remote(ref, ref, z_s.at[0, 2], z_r.at[0, 2], y * X + (x + d) % X, col).start()
            remote(ref, ref, z_s.at[0, 2], z_r.at[0, 2], y * X + (x + d) % X, other).start()

        loop(X, send, 1)
        remote(ref, ref, z_s.at[0, 2], z_r.at[0, 2], row, other).start()

    def z_last(step):
        if step == 0:
            wait(zx.at[pl.ds(0, X * C - 1)], z_r.at[0, 2])
            sums = [z_sum([zx[i * C + c, 0:1, :] for i in range(X)]) for c in range(C)]
        else:
            @pl.when(owner == 1)
            def _():
                wait(zx1.at[pl.ds(0, X - 1)], z_r.at[1, 2])

            @pl.when(owner == 0)
            def _():
                wait(zx1, z_r.at[1, 2])

            sums = [z_sum([zx1[i, c, 0:1, :] for i in range(X)]) for c in range(C)]
        n = HALF // C
        inv = [1.0 / v for v in sums]
        scale = jnp.concatenate([v[:, g * n : (g + 1) * n] for g in range(G) for v in inv], axis=1)
        at_hi[...], at_lo[...] = split(at[step] * scale)

    def counts_part(step, sl):
        return (
            dot(at_hi[...], w_hi[step, sl], NN)
            + dot(at_lo[...], w_hi[step, sl], NN)
            + dot(at_hi[...], w_lo[step, sl], NN)
        )

    def alphas_turned():
        wait(al.at[0, :, 1 - k], ap.at[1])
        for step in range(STEPS):
            v = al[step].reshape(SEQ, RB)
            for i in range(RB // 128):
                at[step, i * 128 : (i + 1) * 128, :] = jnp.transpose(v[:, i * 128 : (i + 1) * 128])

    for g in range(G):
        y_sends(0, g, tsend.at[0, g])
    tsend[1] = emit(1)
    loads[3].wait()
    alpha_1_sends()

    loads[4].wait()

    def split_rows(i):
        r = pl.ds(pl.multiple_of(i * 64, 64), 64)
        hi, lo = split(t_f[r, :])
        t_hi[r, :] = hi
        t_lo[r, :] = lo

    loop(RB // 64, split_rows)

    x_stage(0, 0)
    alpha_step(0)
    x_stage(0, 1)
    alpha_1_on()
    arrivals(0, 0)
    product(0, 0)
    alpha_step(1)
    sums_out(0, 0)
    alpha_transition()
    arrivals(0, 1)
    product(0, 1)
    alpha_step(2)
    sums_out(0, 1)

    next_weighted(0)
    alpha_step(3)
    x_stage(1, 0)
    next_weighted(1)
    alpha_step(4)
    alpha_transition_sum()
    z_part_1(0)
    z_part_0()
    z_first_0()
    x_stage(1, 1)
    z_part_1(1)
    z_first_1()
    alphas_turned()
    arrivals(1, 0)
    product(1, 0)
    z_second_0()
    z_second_1()
    sums_out(1, 0)
    z_third_0()
    arrivals(1, 1)
    product(1, 1)
    z_third_1()
    sums_out(1, 1)

    z_last(0)
    for sl in range(2):
        counts_out[:, sl * RB : (sl + 1) * RB] = counts_part(0, sl)

    for step in range(STEPS):
        for g in range(G):
            wait(cr.at[step, g, pl.ds(0, Y - 1)], y_s.at[step, g, 0])
            wait(cr.at[step, g, pl.ds(0, Z - 1)], c_s.at[step, g])
            wait(pr.at[step, g], p_s.at[step, g])

            @pl.when(owner * diag == 0)
            def _():
                wait(wblk.at[g], y_s.at[step, g, 1])

            @pl.when(owner == 1)
            def _():
                for i in range(X - 1):
                    wait(w.at[step, 0, g], x_s.at[step, g])

    wait(zz.at[0, pl.ds(0, Z - 1)], z_s.at[0, 0])
    wait(zy.at[pl.ds(0, Y - 1)], z_s.at[0, 1])
    wait(zx.at[pl.ds(0, X * C - 1)], z_s.at[0, 2])

    @pl.when(owner == 1)
    def _():
        wait(zz1.at[pl.ds(0, Z - 1)], z_s.at[1, 0])
        wait(zy1.at[pl.ds(0, Y - 1)], z_s.at[1, 1])
        for i in range(X * C - 1):
            wait(zx1.at[0], z_s.at[1, 2])

    for d in (1, 2, 3):
        @pl.when(((x + d) % X) // 2 == k)
        def _():
            wait(g1.at[0], g_s.at[d])

    wait(al.at[1, :, k, pl.ds(0, Z - 1)], b_s.at[0])
    wait(al.at[1, :, k], b_s.at[1])
    for i in range(7):
        wait(al.at[0, :, 0, 0], a_s.at[i])
    wait(al.at[0, :, 0], ap.at[0])

    z_last(1)
    for sl in range(2):
        cols = slice(sl * RB, (sl + 1) * RB)
        counts_out[:, cols] = (t_f[:, cols] * (counts_out[:, cols] + counts_part(1, sl))) * FACTOR
    own = z_sum([zx1[i, k, 0:1, :] for i in range(X)])
    zc[...] = jnp.transpose(jnp.broadcast_to(own, (128, SEQ // C))).reshape(G, Z, T, 128)
    for g in range(G):
        norm = zc[g, z]
        beta_out[g] = (reduced(1, g) / jnp.concatenate([norm] * (RB // 128), axis=1)) * float(H)


def per_device(transition, alphas, beta_last, emission, token_ids):
    hbm = pl.BlockSpec(memory_space=pltpu.HBM)
    vmem = pl.BlockSpec(memory_space=pltpu.VMEM)
    dma = pltpu.SemaphoreType.DMA
    beta, counts = pl.pallas_call(
        kernel,
        out_shape=(
            pltpu.VMEM((G, T, RB), F32),
            pltpu.VMEM((RB, CB), F32),
        ),
        in_specs=[hbm] * 5,
        out_specs=(vmem, vmem),
        scratch_shapes=[
            pltpu.VMEM((RB, CB), F32),
            pltpu.VMEM((RB, CB), BF16),
            pltpu.VMEM((RB, CB), BF16),
            pltpu.VMEM((NCOL, RB), F32),
            pltpu.VMEM((G, T, RB), F32),
            pltpu.VMEM((STEPS, BS), jnp.int32),
            pltpu.VMEM((STEPS, G, C, Z, T, RB), F32),
            pltpu.VMEM((STEPS, RB, SEQ), F32),
            pltpu.VMEM((RB, SEQ), BF16),
            pltpu.VMEM((RB, SEQ), BF16),
            pltpu.VMEM((2, G, T, RB), F32),
            pltpu.VMEM((G, T, RB), F32),
            pltpu.VMEM((STEPS, 2, G, Z, C, T, RB), F32),
            pltpu.VMEM((STEPS, 2, SEQ, RB), BF16),
            pltpu.VMEM((STEPS, 2, SEQ, RB), BF16),
            pltpu.VMEM((STEPS, G, C, Z, T, RB), F32),
            pltpu.VMEM((STEPS, G, Z, T, RB), F32),
            pltpu.VMEM((STEPS, G, Z, T, RB), F32),
            pltpu.VMEM((2, SEQ, RB), F32),
            pltpu.VMEM((X, SEQ, RB), F32),
            pltpu.VMEM((C, G, HALF // C, 128), F32),
            pltpu.VMEM((1, Z, 8, 128), F32),
            pltpu.VMEM((Z, C, 8, 128), F32),
            pltpu.VMEM((Y, 8, 128), F32),
            pltpu.VMEM((Y, C, 8, 128), F32),
            pltpu.VMEM((X * C, 8, 128), F32),
            pltpu.VMEM((X, C, 8, 128), F32),
            pltpu.VMEM((G, Z, T, 128), F32),
            dma((5,)),
            dma((7,)), dma((Z,)),
            dma((2,)),
            dma((2,)), dma((2,)),
            dma((X,)), dma((1,)),
            dma((STEPS, G, 2)), dma((STEPS, G, Y)),
            dma((STEPS, G)), dma((STEPS, G)),
            dma((STEPS, G)), dma((STEPS, G)),
            dma((STEPS, G)), dma((STEPS, G)),
            dma((STEPS, 3)), dma((STEPS, 3)),
        ],
        compiler_params=pltpu.CompilerParams(
            collective_id=0, has_side_effects=True, vmem_limit_bytes=52 * 1024 * 1024
        ),
    )(
        transition,
        alphas.reshape(STEPS, G, T, RB),
        beta_last.reshape(G, T, RB),
        emission,
        token_ids,
    )
    return beta.reshape(BS, RB), counts


def solution(mesh):
    return jax.shard_map(
        per_device,
        mesh=mesh,
        in_specs=(
            P("row", "col"),
            P(None, "col", "row"),
            P("col", "row"),
            P(None, "row"),
            P(None, "col"),
        ),
        out_specs=(P("col", "row"), P("row", "col")),
        check_vma=False,
    )
```

```python
import jax
import jax.numpy as jnp
from jax import lax
from jax.experimental import pallas as pl
from jax.experimental.pallas import tpu as pltpu
from jax.sharding import PartitionSpec as P

H = 16384
STEPS = 2
SEQ = 256
X, Y, Z, C = 4, 8, 8, 2
G = 2
BS = SEQ // (Z * C)
T = BS // G
HALF = SEQ // G
RB = H // (X * Y)
CB = H // (Z * C)
NCOL = 128
FACTOR = float(H * H) / float(SEQ * STEPS)
F32 = jnp.float32
BF16 = jnp.bfloat16
MESH = pl.DeviceIdType.MESH
NT = ((1,), (1,))
NN = ((1,), (0,))


def loop(n, body, start=0):
    def step(i, carry):
        body(i)
        return carry

    lax.fori_loop(start, n, step, 0)


def remote(src, dst, send, recv, row, col):
    return pltpu.make_async_remote_copy(
        src_ref=src, dst_ref=dst, send_sem=send, recv_sem=recv, device_id=(row, col), device_id_type=MESH
    )


def wait(ref, sem):
    pltpu.make_async_copy(ref, ref, sem).wait()


def near_first(j):
    return (j % 2) * ((j + 1) // 2) + (1 - j % 2) * (8 - j // 2)


def split(v):
    hi = v.astype(BF16)
    return hi, (v - hi.astype(F32)).astype(BF16)


def dot(a, b, dims):
    return lax.dot_general(a, b, (dims, ((), ())), preferred_element_type=F32)


def kernel(
    trans_hbm, alphas_hbm, beta_hbm, emis_hbm, tok_hbm,
    beta_out, counts_out,
    t_f, t_hi, t_lo, emis, beta0, tok, al, at, at_hi, at_lo, tsend, wblk, st, w, w_hi, w_lo, ub, pr, cr, g1, gx, zpart, zz, zy, zx, zc,
    ld, a_s, a_r, ap, b_s, b_r, g_s, g_r, y_s, y_r, x_s, x_r, p_s, p_r, c_s, c_r, z_s, z_r,
):
    row = lax.axis_index("row")
    col = lax.axis_index("col")
    x, y, z, k = row % X, row // X, col // C, col % C
    kd = x // 2
    slot = x % 2
    fslot = 1 - slot
    other = z * C + 1 - k

    loads = [
        pltpu.make_async_copy(tok_hbm, tok, ld.at[0]),
        pltpu.make_async_copy(emis_hbm, emis, ld.at[1]),
        pltpu.make_async_copy(beta_hbm, beta0, ld.at[2]),
        pltpu.make_async_copy(alphas_hbm, al.at[:, :, k, z], ld.at[3]),
        pltpu.make_async_copy(trans_hbm, t_f, ld.at[4]),
    ]
    for c in loads:
        c.start()

    bar = pltpu.get_barrier_semaphore()

    def greet(r, c):
        pl.semaphore_signal(bar, inc=1, device_id=(r, c), device_id_type=MESH)

    owner = 1 - (k + kd) % 2
    diag = 1 - ((y - z + Z) % Z + Z - 1) // Z

    def greet_cross(d):
        greet(((y + d) % Y) * X + x, y * C + k)
        greet(z * X + x, ((z + d) % Z) * C + k)

    def greet_lines(d):
        greet(row, ((z + d) % Z) * C + k)
        greet(((y + d) % Y) * X + x, col)

    def greet_x(d):
        greet(y * X + (x + d) % X, col)
        greet(y * X + (x + d) % X, other)

    loop(Z, greet_cross, 1)

    @pl.when(diag == 0)
    def _():
        greet(row, y * C + k)
        greet(z * X + x, col)

    loop(Z, greet_lines, 1)
    loop(X, greet_x, 1)
    greet(row, other)

    loads[0].wait()
    loads[1].wait()
    labels = lax.broadcasted_iota(jnp.int32, (NCOL, BS), 0)
    em = emis[...]

    def emit(step):
        onehot = (labels == tok[step : step + 1, :]).astype(F32)
        out = lax.dot_general(
            onehot, em, (((0,), (0,)), ((), ())), precision=lax.Precision.HIGHEST, preferred_element_type=F32
        )
        return out.reshape(G, T, RB)

    loads[2].wait()
    tsend[0] = emit(0) * beta0[...]

    pl.semaphore_wait(bar, 2 * (Z - 1) + 2 * (X - 1) + 1 + 2 * (Z - diag))

    def alpha_1_sends():
        ref = al.at[1, :, k, z]

        def send(d):
            remote(ref, ref, b_s.at[0], b_r.at[0], row, ((z + d) % Z) * C + k).start()

        loop(Z, send, 1)

    def alpha_1_on():
        wait(al.at[1, :, k, pl.ds(0, Z - 1)], b_r.at[0])
        half = al.at[1, :, k]
        remote(half, half, b_s.at[1], b_r.at[1], row, other).start()

    def alpha_step(i):
        if i < 4:
            b = (z - i + Z) % Z
            ref = al.at[0, :, k, b]
            if i:
                wait(ref, a_r.at[b])
            remote(ref, ref, a_s.at[i], a_r.at[b], row, ((z + 1) % Z) * C + k).start()
        if i < 3:
            b = (z + i) % Z
            ref = al.at[0, :, k, b]
            if i:
                wait(ref, a_r.at[b])
            remote(ref, ref, a_s.at[4 + i], a_r.at[b], row, ((z + Z - 1) % Z) * C + k).start()
        if i == 4:
            for b in ((z + 4) % Z, (z + 3) % Z):
                wait(al.at[0, :, k, b], a_r.at[b])
            half = al.at[0, :, k]
            remote(half, half, ap.at[0], ap.at[1], row, other).start()

    def y_sends(step, g, src):
        recv = y_r.at[step, g, z]

        def send_to(dst):
            def send(j):
                to = (y + near_first(Y - j)) % Y
                remote(src, dst, y_s.at[step, g, 0], recv, to * X + x, y * C + k).start()

            loop(Y, send, 1)

            @pl.when(diag == 1)
            def _():
                pltpu.make_async_copy(src, dst, recv).start()

            @pl.when(diag == 0)
            def _():
                remote(src, dst, y_s.at[step, g, 1], recv, row, y * C + k).start()

        @pl.when(owner == 1)
        def _():
            send_to(w.at[step, slot, g, z, k])

        @pl.when(owner == 0)
        def _():
            send_to(st.at[step, g, z])

    def x_stage(step, g):
        def sends(here, block):
            def send(j):
                s = (z + near_first(j)) % Z
                src = block(s)
                dst = w.at[step, slot, g, s, k]
                wait(src, y_r.at[step, g, s])
                for d in (2, 1, 3):
                    remote(src, dst, x_s.at[step, g], x_r.at[step, g], y * X + (x + d) % X, z * C + kd).start()
                if here:
                    remote(src, dst, x_s.at[step, g], x_r.at[step, g], row, other).start()

            loop(Z, send)

        @pl.when(owner == 1)
        def _():
            sends(False, lambda s: w.at[step, slot, g, s, k])

        @pl.when(owner == 0)
        def _():
            sends(True, lambda s: st.at[step, g, s])

    def wait_x(step, g, sem):
        @pl.when(owner == 1)
        def _():
            wait(w.at[step, :, g, pl.ds(0, 3 * Z // 4)], sem)

        @pl.when(owner == 0)
        def _():
            wait(w.at[step, :, g], sem)

    def arrivals(step, g):
        wait_x(step, g, x_r.at[step, g])

    def product(step, g):
        acc = None
        for sl in range(2):
            hi, lo = split(jnp.concatenate([w[step, sl, g, :, c].reshape(HALF // C, RB) for c in range(C)], axis=0))
            w_hi[step, sl, g * HALF : (g + 1) * HALF, :] = hi
            w_lo[step, sl, g * HALF : (g + 1) * HALF, :] = lo
            cols = slice(sl * RB, (sl + 1) * RB)
            both = dot(jnp.concatenate([hi, lo], axis=0), t_hi[:, cols], NT)
            part = both[:HALF] + both[HALF:] + dot(hi, t_lo[:, cols], NT)
            acc = part if acc is None else acc + part
        ub[step, g] = acc.reshape(C, Z, T, RB)
        remote(ub.at[step, g, 1 - k], pr.at[step, g], p_s.at[step, g], p_r.at[step, g], row, other).start()

    def sums_out(step, g):
        wait(pr.at[step, g], p_r.at[step, g])
        ub[step, g, k] = ub[step, g, k] + pr[step, g]
        dst = cr.at[step, g, z]
        recv = c_r.at[step, g]

        def send(j):
            s = (z + near_first(Z - j)) % Z
            remote(ub.at[step, g, k, s], dst, c_s.at[step, g], recv, row, s * C + k).start()

        loop(Z, send, 1)
        pltpu.make_async_copy(ub.at[step, g, k, z], dst, recv).start()

    def reduced(step, g):
        wait(cr.at[step, g], c_r.at[step, g])
        acc = cr[step, g, 0]
        for i in range(1, Z):
            acc = acc + cr[step, g, i]
        return acc

    def next_weighted(g):
        wblk[g] = reduced(0, g) * tsend[1, g]
        y_sends(1, g, wblk.at[g])

    def lanes(parts):
        acc = None
        for v in parts:
            for i in range(RB // 128):
                t = v[:, i * 128 : (i + 1) * 128]
                acc = t if acc is None else acc + t
        return acc

    def z_part_0():
        v = (ub[0, :, k] * al[0, :, k]).reshape(SEQ // C, RB)
        zz[0, z] = z_row(lanes([v]))
        z_first(0)

    def z_row(part):
        return jnp.broadcast_to(jnp.sum(jnp.transpose(part), axis=0, keepdims=True), (8, SEQ // C))

    def z_first(step):
        if step:
            zz[1, z] = z_row(zpart[...].reshape(SEQ // C, 128))

        def send(d):
            ref = zz.at[step, z]
            remote(ref, ref, z_s.at[step, 0], z_r.at[step, 0], row, ((z + d) % Z) * C + k).start()

        loop(Z, send, 1)

    def alpha_transition():
        wait(al.at[1, :, 1 - k], b_r.at[1])
        n = HALF // C
        a_hi, a_lo = split(
            jnp.concatenate([al[1, g, c].reshape(n, RB) for c in range(C) for g in range(G)], axis=0)
        )
        for sl in range(2):
            cols = slice(sl * RB, (sl + 1) * RB)
            v = dot(a_hi, t_hi[:, cols], NN) + dot(a_lo, t_hi[:, cols], NN) + dot(a_hi, t_lo[:, cols], NN)
            g1[sl] = v.reshape(C, G, n, RB)

        for d in (2, 1, 3):
            to = (x + d) % X

            @pl.when(to // 2 == k)
            def _():
                for c in range(C):
                    remote(g1.at[to % 2, c], gx.at[x], g_s.at[d, c], g_r.at[0], y * X + to, z * C + c).start()

        @pl.when(owner == 1)
        def _():
            pltpu.make_async_copy(g1.at[slot, k], gx.at[x], g_r.at[0]).start()
            remote(g1.at[slot, 1 - k], gx.at[x], g_s.at[0, 0], g_r.at[0], row, other).start()

    def alpha_transition_sum():
        wait(gx, g_r.at[0])
        gx[0] = z_sum([gx[i] for i in range(X)])

    def z_part_1(g):
        n = HALF // C

        @pl.when(owner == 1)
        def _():
            zpart[g] = lanes([gx[0, g] * w[1, slot, g, :, k].reshape(n, RB)])

        @pl.when(owner == 0)
        def _():
            zpart[g] = lanes([gx[0, g] * st[1, g].reshape(n, RB)])

    def z_sum(parts):
        v = parts[0]
        for p in parts[1:]:
            v = v + p
        return v

    def z_second(step):
        wait(zz.at[step, pl.ds(0, Z - 1)], z_r.at[step, 0])
        zy[step, y] = z_sum([zz[step, i] for i in range(Z)])

        def send(d):
            ref = zy.at[step, y]
            remote(ref, ref, z_s.at[step, 1], z_r.at[step, 1], ((y + d) % Y) * X + x, col).start()

        loop(Y, send, 1)

    def z_third(step):
        wait(zy.at[step, pl.ds(0, Y - 1)], z_r.at[step, 1])
        zx[step, x * C + k] = z_sum([zy[step, i] for i in range(Y)])
        ref = zx.at[step, x * C + k]

        def send(d):
            remote(ref, ref, z_s.at[step, 2], z_r.at[step, 2], y * X + (x + d) % X, col).start()
            remote(ref, ref, z_s.at[step, 2], z_r.at[step, 2], y * X + (x + d) % X, other).start()

        loop(X, send, 1)
        remote(ref, ref, z_s.at[step, 2], z_r.at[step, 2], row, other).start()

    def z_last(step):
        wait(zx.at[step, pl.ds(0, X * C - 1)], z_r.at[step, 2])
        sums = [z_sum([zx[step, i * C + c, 0:1, :] for i in range(X)]) for c in range(C)]
        n = HALF // C
        inv = [1.0 / v for v in sums]
        scale = jnp.concatenate([v[:, g * n : (g + 1) * n] for g in range(G) for v in inv], axis=1)
        at_hi[...], at_lo[...] = split(at[step] * scale)

    def counts_part(step, sl):
        return (
            dot(at_hi[...], w_hi[step, sl], NN)
            + dot(at_lo[...], w_hi[step, sl], NN)
            + dot(at_hi[...], w_lo[step, sl], NN)
        )

    def alphas_turned():
        wait(al.at[0, :, 1 - k], ap.at[1])
        for step in range(STEPS):
            v = al[step].reshape(SEQ, RB)
            for i in range(RB // 128):
                at[step, i * 128 : (i + 1) * 128, :] = jnp.transpose(v[:, i * 128 : (i + 1) * 128])

    for g in range(G):
        y_sends(0, g, tsend.at[0, g])
    tsend[1] = emit(1)
    loads[3].wait()
    alpha_1_sends()

    loads[4].wait()

    def split_rows(i):
        r = pl.ds(pl.multiple_of(i * 64, 64), 64)
        hi, lo = split(t_f[r, :])
        t_hi[r, :] = hi
        t_lo[r, :] = lo

    loop(RB // 64, split_rows)

    x_stage(0, 0)
    alpha_step(0)
    x_stage(0, 1)
    alpha_1_on()
    arrivals(0, 0)
    product(0, 0)
    alpha_step(1)
    sums_out(0, 0)
    alpha_transition()
    arrivals(0, 1)
    product(0, 1)
    alpha_step(2)
    sums_out(0, 1)

    next_weighted(0)
    alpha_step(3)
    x_stage(1, 0)
    next_weighted(1)
    alpha_step(4)
    alpha_transition_sum()
    z_part_1(0)
    z_part_0()
    x_stage(1, 1)
    z_part_1(1)
    z_first(1)
    alphas_turned()
    arrivals(1, 0)
    product(1, 0)
    z_second(0)
    z_second(1)
    sums_out(1, 0)
    z_third(0)
    arrivals(1, 1)
    product(1, 1)
    z_third(1)
    sums_out(1, 1)

    z_last(0)
    for sl in range(2):
        counts_out[:, sl * RB : (sl + 1) * RB] = counts_part(0, sl)

    for step in range(STEPS):
        for g in range(G):
            wait(cr.at[step, g, pl.ds(0, Y - 1)], y_s.at[step, g, 0])
            wait(cr.at[step, g, pl.ds(0, Z - 1)], c_s.at[step, g])
            wait(pr.at[step, g], p_s.at[step, g])

            @pl.when(diag == 0)
            def _():
                wait(wblk.at[g], y_s.at[step, g, 1])

            wait_x(step, g, x_s.at[step, g])

        wait(zz.at[0, pl.ds(0, Z - 1)], z_s.at[step, 0])
        wait(zz.at[0, pl.ds(0, Y - 1)], z_s.at[step, 1])
        wait(zz.at[0, pl.ds(0, X * C - 1)], z_s.at[step, 2])

    for d in (1, 2, 3):
        @pl.when(((x + d) % X) // 2 == k)
        def _():
            for c in range(C):
                wait(gx.at[0], g_s.at[d, c])

    @pl.when(owner == 1)
    def _():
        wait(gx.at[0], g_s.at[0, 0])

    wait(al.at[1, :, k, pl.ds(0, Z - 1)], b_s.at[0])
    wait(al.at[1, :, k], b_s.at[1])
    for i in range(7):
        wait(al.at[0, :, 0, 0], a_s.at[i])
    wait(al.at[0, :, 0], ap.at[0])

    z_last(1)
    for sl in range(2):
        cols = slice(sl * RB, (sl + 1) * RB)
        counts_out[:, cols] = (t_f[:, cols] * (counts_out[:, cols] + counts_part(1, sl))) * FACTOR
    own = z_sum([zx[1, i * C + k, 0:1, :] for i in range(X)])
    zc[...] = jnp.transpose(jnp.broadcast_to(own, (128, SEQ // C))).reshape(G, Z, T, 128)
    for g in range(G):
        norm = zc[g, z]
        beta_out[g] = (reduced(1, g) / jnp.concatenate([norm] * (RB // 128), axis=1)) * float(H)


def per_device(transition, alphas, beta_last, emission, token_ids):
    hbm = pl.BlockSpec(memory_space=pltpu.HBM)
    vmem = pl.BlockSpec(memory_space=pltpu.VMEM)
    dma = pltpu.SemaphoreType.DMA
    beta, counts = pl.pallas_call(
        kernel,
        out_shape=(
            pltpu.VMEM((G, T, RB), F32),
            pltpu.VMEM((RB, CB), F32),
        ),
        in_specs=[hbm] * 5,
        out_specs=(vmem, vmem),
        scratch_shapes=[
            pltpu.VMEM((RB, CB), F32),
            pltpu.VMEM((RB, CB), BF16),
            pltpu.VMEM((RB, CB), BF16),
            pltpu.VMEM((NCOL, RB), F32),
            pltpu.VMEM((G, T, RB), F32),
            pltpu.VMEM((STEPS, BS), jnp.int32),
            pltpu.VMEM((STEPS, G, C, Z, T, RB), F32),
            pltpu.VMEM((STEPS, RB, SEQ), F32),
            pltpu.VMEM((RB, SEQ), BF16),
            pltpu.VMEM((RB, SEQ), BF16),
            pltpu.VMEM((2, G, T, RB), F32),
            pltpu.VMEM((G, T, RB), F32),
            pltpu.VMEM((STEPS, G, Z, T, RB), F32),
            pltpu.VMEM((STEPS, 2, G, Z, C, T, RB), F32),
            pltpu.VMEM((STEPS, 2, SEQ, RB), BF16),
            pltpu.VMEM((STEPS, 2, SEQ, RB), BF16),
            pltpu.VMEM((STEPS, G, C, Z, T, RB), F32),
            pltpu.VMEM((STEPS, G, Z, T, RB), F32),
            pltpu.VMEM((STEPS, G, Z, T, RB), F32),
            pltpu.VMEM((2, C, G, HALF // C, RB), F32),
            pltpu.VMEM((X, G, HALF // C, RB), F32),
            pltpu.VMEM((G, HALF // C, 128), F32),
            pltpu.VMEM((STEPS, Z, 8, 128), F32),
            pltpu.VMEM((STEPS, Y, 8, 128), F32),
            pltpu.VMEM((STEPS, X * C, 8, 128), F32),
            pltpu.VMEM((G, Z, T, 128), F32),
            dma((5,)),
            dma((7,)), dma((Z,)),
            dma((2,)),
            dma((2,)), dma((2,)),
            dma((X, C)), dma((1,)),
            dma((STEPS, G, 2)), dma((STEPS, G, Y)),
            dma((STEPS, G)), dma((STEPS, G)),
            dma((STEPS, G)), dma((STEPS, G)),
            dma((STEPS, G)), dma((STEPS, G)),
            dma((STEPS, 3)), dma((STEPS, 3)),
        ],
        compiler_params=pltpu.CompilerParams(
            collective_id=0, has_side_effects=True, vmem_limit_bytes=52 * 1024 * 1024
        ),
    )(
        transition,
        alphas.reshape(STEPS, G, T, RB),
        beta_last.reshape(G, T, RB),
        emission,
        token_ids,
    )
    return beta.reshape(BS, RB), counts


def solution(mesh):
    return jax.shard_map(
        per_device,
        mesh=mesh,
        in_specs=(
            P("row", "col"),
            P(None, "col", "row"),
            P("col", "row"),
            P(None, "row"),
            P(None, "col"),
        ),
        out_specs=(P("col", "row"), P("row", "col")),
        check_vma=False,
    )
```

```python
import jax
import jax.numpy as jnp
from jax import lax
from jax.experimental import pallas as pl
from jax.experimental.pallas import tpu as pltpu
from jax.sharding import PartitionSpec as P

H = 16384
STEPS = 2
SEQ = 256
X, Y, Z, C = 4, 8, 8, 2
G = 2
BS = SEQ // (Z * C)
T = BS // G
HALF = SEQ // G
RB = H // (X * Y)
CB = H // (Z * C)
NCOL = 128
FACTOR = float(H * H) / float(SEQ * STEPS)
F32 = jnp.float32
BF16 = jnp.bfloat16
MESH = pl.DeviceIdType.MESH
NT = ((1,), (1,))
NN = ((1,), (0,))


def loop(n, body, start=0):
    def step(i, carry):
        body(i)
        return carry

    lax.fori_loop(start, n, step, 0)


def remote(src, dst, send, recv, row, col):
    return pltpu.make_async_remote_copy(
        src_ref=src, dst_ref=dst, send_sem=send, recv_sem=recv, device_id=(row, col), device_id_type=MESH
    )


def wait(ref, sem):
    pltpu.make_async_copy(ref, ref, sem).wait()


def near_first(j):
    return (j % 2) * ((j + 1) // 2) + (1 - j % 2) * (8 - j // 2)


def split(v):
    hi = v.astype(BF16)
    return hi, (v - hi.astype(F32)).astype(BF16)


def dot(a, b, dims):
    return lax.dot_general(a, b, (dims, ((), ())), preferred_element_type=F32)


def kernel(
    trans_hbm, alphas_hbm, beta_hbm, emis_hbm, tok_hbm,
    beta_out, counts_out,
    t_f, t_hi, t_lo, emis, beta0, tok, al, at, at_hi, at_lo, tsend, wblk, st, w, w_hi, w_lo, ub, pr, cr, g1, gx, zpart, zz, zy, zx, zc,
    ld, a_s, a_r, ap, b_s, b_r, g_s, g_r, y_s, y_r, x_s, x_r, p_s, p_r, c_s, c_r, z_s, z_r,
):
    row = lax.axis_index("row")
    col = lax.axis_index("col")
    x, y, z, k = row % X, row // X, col // C, col % C
    kd = x // 2
    slot = x % 2
    fslot = 1 - slot
    other = z * C + 1 - k

    bar = pltpu.get_barrier_semaphore()

    def greet(r, c):
        pl.semaphore_signal(bar, inc=1, device_id=(r, c), device_id_type=MESH)

    owner = 1 - (k + kd) % 2
    diag = 1 - ((y - z + Z) % Z + Z - 1) // Z

    def greet_cross(d):
        greet(((y + d) % Y) * X + x, y * C + k)
        greet(z * X + x, ((z + d) % Z) * C + k)

    def greet_lines(d):
        greet(row, ((z + d) % Z) * C + k)
        greet(((y + d) % Y) * X + x, col)

    def greet_x(d):
        greet(y * X + (x + d) % X, col)
        greet(y * X + (x + d) % X, other)

    loop(Z, greet_cross, 1)

    @pl.when(diag == 0)
    def _():
        greet(row, y * C + k)
        greet(z * X + x, col)

    loop(Z, greet_lines, 1)
    loop(X, greet_x, 1)
    greet(row, other)

    loads = [
        pltpu.make_async_copy(tok_hbm, tok, ld.at[0]),
        pltpu.make_async_copy(emis_hbm, emis, ld.at[1]),
        pltpu.make_async_copy(beta_hbm, beta0, ld.at[2]),
        pltpu.make_async_copy(alphas_hbm, al.at[:, :, k, z], ld.at[3]),
        pltpu.make_async_copy(trans_hbm, t_f, ld.at[4]),
    ]
    for c in loads:
        c.start()

    loads[0].wait()
    loads[1].wait()
    labels = lax.broadcasted_iota(jnp.int32, (NCOL, BS), 0)
    em = emis[...]

    def emit(step):
        onehot = (labels == tok[step : step + 1, :]).astype(F32)
        out = lax.dot_general(
            onehot, em, (((0,), (0,)), ((), ())), precision=lax.Precision.HIGHEST, preferred_element_type=F32
        )
        return out.reshape(G, T, RB)

    loads[2].wait()
    tsend[0] = emit(0) * beta0[...]

    pl.semaphore_wait(bar, 2 * (Z - 1) + 2 * (X - 1) + 1 + 2 * (Z - diag))

    def alpha_1_sends():
        ref = al.at[1, :, k, z]

        def send(d):
            remote(ref, ref, b_s.at[0], b_r.at[0], row, ((z + d) % Z) * C + k).start()

        loop(Z, send, 1)

    def alpha_1_on():
        wait(al.at[1, :, k, pl.ds(0, Z - 1)], b_r.at[0])
        half = al.at[1, :, k]
        remote(half, half, b_s.at[1], b_r.at[1], row, other).start()

    def alpha_step(i):
        if i < 4:
            b = (z - i + Z) % Z
            ref = al.at[0, :, k, b]
            if i:
                wait(ref, a_r.at[b])
            remote(ref, ref, a_s.at[i], a_r.at[b], row, ((z + 1) % Z) * C + k).start()
        if i < 3:
            b = (z + i) % Z
            ref = al.at[0, :, k, b]
            if i:
                wait(ref, a_r.at[b])
            remote(ref, ref, a_s.at[4 + i], a_r.at[b], row, ((z + Z - 1) % Z) * C + k).start()
        if i == 4:
            for b in ((z + 4) % Z, (z + 3) % Z):
                wait(al.at[0, :, k, b], a_r.at[b])
            half = al.at[0, :, k]
            remote(half, half, ap.at[0], ap.at[1], row, other).start()

    def y_sends(step, g, src):
        recv = y_r.at[step, g, z]

        def send_to(dst):
            def send(j):
                to = (y + near_first(Y - j)) % Y
                remote(src, dst, y_s.at[step, g, 0], recv, to * X + x, y * C + k).start()

            loop(Y, send, 1)

            @pl.when(diag == 1)
            def _():
                pltpu.make_async_copy(src, dst, recv).start()

            @pl.when(diag == 0)
            def _():
                remote(src, dst, y_s.at[step, g, 1], recv, row, y * C + k).start()

        @pl.when(owner == 1)
        def _():
            send_to(w.at[step, slot, g, z, k])

        @pl.when(owner == 0)
        def _():
            send_to(st.at[step, g, z])

    def x_stage(step, g, start=0, stop=Z // 2):
        def sends(here, block):
            def send(j):
                s = (z // 2 + (j % 2) * ((j + 1) // 2) + (1 - j % 2) * (4 - j // 2)) % 4 * 2
                for i in range(2):
                    wait(block(s + i), y_r.at[step, g, s + i])
                src = block(pl.ds(s, 2))
                dst = w.at[step, slot, g, pl.ds(s, 2), k]
                for d in (2, 1, 3):
                    remote(src, dst, x_s.at[step, g], x_r.at[step, g], y * X + (x + d) % X, z * C + kd).start()
                if here:
                    remote(src, dst, x_s.at[step, g], x_r.at[step, g], row, other).start()

            loop(stop, send, start)

        @pl.when(owner == 1)
        def _():
            sends(False, lambda s: w.at[step, slot, g, s, k])

        @pl.when(owner == 0)
        def _():
            sends(True, lambda s: st.at[step, g, s])

    def wait_x(step, g, sem):
        @pl.when(owner == 1)
        def _():
            wait(w.at[step, :, g, pl.ds(0, 3 * Z // 4)], sem)

        @pl.when(owner == 0)
        def _():
            wait(w.at[step, :, g], sem)

    def arrivals(step, g):
        wait_x(step, g, x_r.at[step, g])

    def product(step, g):
        acc = None
        for sl in range(2):
            hi, lo = split(jnp.concatenate([w[step, sl, g, :, c].reshape(HALF // C, RB) for c in range(C)], axis=0))
            w_hi[step, sl, g * HALF : (g + 1) * HALF, :] = hi
            w_lo[step, sl, g * HALF : (g + 1) * HALF, :] = lo
            cols = slice(sl * RB, (sl + 1) * RB)
            both = dot(jnp.concatenate([hi, lo], axis=0), t_hi[:, cols], NT)
            part = both[:HALF] + both[HALF:] + dot(hi, t_lo[:, cols], NT)
            acc = part if acc is None else acc + part
        ub[step, g] = acc.reshape(C, Z, T, RB)
        remote(ub.at[step, g, 1 - k], pr.at[step, g], p_s.at[step, g], p_r.at[step, g], row, other).start()

    def sums_out(step, g):
        wait(pr.at[step, g], p_r.at[step, g])
        ub[step, g, k] = ub[step, g, k] + pr[step, g]
        dst = cr.at[step, g, z]
        recv = c_r.at[step, g]

        def send(j):
            s = (z + near_first(Z - j)) % Z
            remote(ub.at[step, g, k, s], dst, c_s.at[step, g], recv, row, s * C + k).start()

        loop(Z, send, 1)
        pltpu.make_async_copy(ub.at[step, g, k, z], dst, recv).start()

    def reduced(step, g):
        wait(cr.at[step, g], c_r.at[step, g])
        acc = cr[step, g, 0]
        for i in range(1, Z):
            acc = acc + cr[step, g, i]
        return acc

    def next_weighted(g):
        wblk[g] = reduced(0, g) * tsend[1, g]
        y_sends(1, g, wblk.at[g])

    def lanes(parts):
        acc = None
        for v in parts:
            for i in range(RB // 128):
                t = v[:, i * 128 : (i + 1) * 128]
                acc = t if acc is None else acc + t
        return acc

    def z_part_0():
        v = (ub[0, :, k] * al[0, :, k]).reshape(SEQ // C, RB)
        zz[0, z] = z_row(lanes([v]))
        z_first(0)

    def z_row(part):
        return jnp.broadcast_to(jnp.sum(jnp.transpose(part), axis=0, keepdims=True), (8, SEQ // C))

    def z_first(step):
        if step:
            zz[1, z] = z_row(zpart[...].reshape(SEQ // C, 128))

        def send(d):
            ref = zz.at[step, z]
            remote(ref, ref, z_s.at[step, 0], z_r.at[step, 0], row, ((z + d) % Z) * C + k).start()

        loop(Z, send, 1)

    def alpha_transition():
        wait(al.at[1, :, 1 - k], b_r.at[1])
        n = HALF // C
        a_hi, a_lo = split(
            jnp.concatenate([al[1, g, c].reshape(n, RB) for c in range(C) for g in range(G)], axis=0)
        )
        for sl in range(2):
            cols = slice(sl * RB, (sl + 1) * RB)
            v = dot(a_hi, t_hi[:, cols], NN) + dot(a_lo, t_hi[:, cols], NN) + dot(a_hi, t_lo[:, cols], NN)
            g1[sl] = v.reshape(C, G, n, RB)

        for d in (2, 1, 3):
            to = (x + d) % X

            @pl.when(to // 2 == k)
            def _():
                for c in range(C):
                    remote(g1.at[to % 2, c], gx.at[x], g_s.at[d, c], g_r.at[0], y * X + to, z * C + c).start()

        @pl.when(owner == 1)
        def _():
            pltpu.make_async_copy(g1.at[slot, k], gx.at[x], g_r.at[0]).start()
            remote(g1.at[slot, 1 - k], gx.at[x], g_s.at[0, 0], g_r.at[0], row, other).start()

    def alpha_transition_sum():
        wait(gx, g_r.at[0])
        gx[0] = z_sum([gx[i] for i in range(X)])

    def z_part_1(g):
        n = HALF // C

        @pl.when(owner == 1)
        def _():
            zpart[g] = lanes([gx[0, g] * w[1, slot, g, :, k].reshape(n, RB)])

        @pl.when(owner == 0)
        def _():
            zpart[g] = lanes([gx[0, g] * st[1, g].reshape(n, RB)])

    def z_sum(parts):
        v = parts[0]
        for p in parts[1:]:
            v = v + p
        return v

    def z_second(step):
        wait(zz.at[step, pl.ds(0, Z - 1)], z_r.at[step, 0])
        zy[step, y] = z_sum([zz[step, i] for i in range(Z)])

        def send(d):
            ref = zy.at[step, y]
            remote(ref, ref, z_s.at[step, 1], z_r.at[step, 1], ((y + d) % Y) * X + x, col).start()

        loop(Y, send, 1)

    def z_third(step):
        wait(zy.at[step, pl.ds(0, Y - 1)], z_r.at[step, 1])
        zx[step, x * C + k] = z_sum([zy[step, i] for i in range(Y)])
        ref = zx.at[step, x * C + k]

        def send(d):
            remote(ref, ref, z_s.at[step, 2], z_r.at[step, 2], y * X + (x + d) % X, col).start()
            remote(ref, ref, z_s.at[step, 2], z_r.at[step, 2], y * X + (x + d) % X, other).start()

        loop(X, send, 1)
        remote(ref, ref, z_s.at[step, 2], z_r.at[step, 2], row, other).start()

    def z_last(step):
        wait(zx.at[step, pl.ds(0, X * C - 1)], z_r.at[step, 2])
        sums = [z_sum([zx[step, i * C + c, 0:1, :] for i in range(X)]) for c in range(C)]
        n = HALF // C
        inv = [1.0 / v for v in sums]
        scale = jnp.concatenate([v[:, g * n : (g + 1) * n] for g in range(G) for v in inv], axis=1)
        at_hi[...], at_lo[...] = split(at[step] * scale)

    def counts_part(step, sl):
        return (
            dot(at_hi[...], w_hi[step, sl], NN)
            + dot(at_lo[...], w_hi[step, sl], NN)
            + dot(at_hi[...], w_lo[step, sl], NN)
        )

    def alphas_turned():
        wait(al.at[0, :, 1 - k], ap.at[1])
        for step in range(STEPS):
            v = al[step].reshape(SEQ, RB)
            for i in range(RB // 128):
                at[step, i * 128 : (i + 1) * 128, :] = jnp.transpose(v[:, i * 128 : (i + 1) * 128])

    for g in range(G):
        y_sends(0, g, tsend.at[0, g])
    tsend[1] = emit(1)
    loads[3].wait()
    alpha_1_sends()

    loads[4].wait()

    def split_rows(i):
        r = pl.ds(pl.multiple_of(i * 64, 64), 64)
        hi, lo = split(t_f[r, :])
        t_hi[r, :] = hi
        t_lo[r, :] = lo

    loop(RB // 64, split_rows)

    x_stage(0, 0)
    alpha_step(0)
    x_stage(0, 1)
    alpha_1_on()
    arrivals(0, 0)
    product(0, 0)
    alpha_step(1)
    sums_out(0, 0)
    alpha_transition()
    arrivals(0, 1)
    product(0, 1)
    alpha_step(2)
    sums_out(0, 1)

    next_weighted(0)
    alpha_step(3)
    x_stage(1, 0, 0, 2)
    next_weighted(1)
    x_stage(1, 0, 2)
    alpha_step(4)
    z_part_0()
    x_stage(1, 1, 0, 2)
    alpha_transition_sum()
    z_part_1(0)
    x_stage(1, 1, 2)
    z_part_1(1)
    z_first(1)
    z_second(0)
    arrivals(1, 0)
    product(1, 0)
    sums_out(1, 0)
    alphas_turned()
    z_third(0)
    z_second(1)
    arrivals(1, 1)
    product(1, 1)
    sums_out(1, 1)
    z_third(1)

    z_last(0)
    for sl in range(2):
        counts_out[:, sl * RB : (sl + 1) * RB] = counts_part(0, sl)

    for step in range(STEPS):
        for g in range(G):
            wait(cr.at[step, g, pl.ds(0, Y - 1)], y_s.at[step, g, 0])
            wait(cr.at[step, g, pl.ds(0, Z - 1)], c_s.at[step, g])
            wait(pr.at[step, g], p_s.at[step, g])

            @pl.when(diag == 0)
            def _():
                wait(wblk.at[g], y_s.at[step, g, 1])

            wait_x(step, g, x_s.at[step, g])

        wait(zz.at[0, pl.ds(0, Z - 1)], z_s.at[step, 0])
        wait(zz.at[0, pl.ds(0, Y - 1)], z_s.at[step, 1])
        wait(zz.at[0, pl.ds(0, X * C - 1)], z_s.at[step, 2])

    for d in (1, 2, 3):
        @pl.when(((x + d) % X) // 2 == k)
        def _():
            for c in range(C):
                wait(gx.at[0], g_s.at[d, c])

    @pl.when(owner == 1)
    def _():
        wait(gx.at[0], g_s.at[0, 0])

    wait(al.at[1, :, k, pl.ds(0, Z - 1)], b_s.at[0])
    wait(al.at[1, :, k], b_s.at[1])
    for i in range(7):
        wait(al.at[0, :, 0, 0], a_s.at[i])
    wait(al.at[0, :, 0], ap.at[0])

    z_last(1)
    for sl in range(2):
        cols = slice(sl * RB, (sl + 1) * RB)
        counts_out[:, cols] = (t_f[:, cols] * (counts_out[:, cols] + counts_part(1, sl))) * FACTOR
    own = z_sum([zx[1, i * C + k, 0:1, :] for i in range(X)])
    zc[...] = jnp.transpose(jnp.broadcast_to(own, (128, SEQ // C))).reshape(G, Z, T, 128)
    for g in range(G):
        norm = zc[g, z]
        beta_out[g] = (reduced(1, g) / jnp.concatenate([norm] * (RB // 128), axis=1)) * float(H)


def per_device(transition, alphas, beta_last, emission, token_ids):
    hbm = pl.BlockSpec(memory_space=pltpu.HBM)
    vmem = pl.BlockSpec(memory_space=pltpu.VMEM)
    dma = pltpu.SemaphoreType.DMA
    beta, counts = pl.pallas_call(
        kernel,
        out_shape=(
            pltpu.VMEM((G, T, RB), F32),
            pltpu.VMEM((RB, CB), F32),
        ),
        in_specs=[hbm] * 5,
        out_specs=(vmem, vmem),
        scratch_shapes=[
            pltpu.VMEM((RB, CB), F32),
            pltpu.VMEM((RB, CB), BF16),
            pltpu.VMEM((RB, CB), BF16),
            pltpu.VMEM((NCOL, RB), F32),
            pltpu.VMEM((G, T, RB), F32),
            pltpu.VMEM((STEPS, BS), jnp.int32),
            pltpu.VMEM((STEPS, G, C, Z, T, RB), F32),
            pltpu.VMEM((STEPS, RB, SEQ), F32),
            pltpu.VMEM((RB, SEQ), BF16),
            pltpu.VMEM((RB, SEQ), BF16),
            pltpu.VMEM((2, G, T, RB), F32),
            pltpu.VMEM((G, T, RB), F32),
            pltpu.VMEM((STEPS, G, Z, T, RB), F32),
            pltpu.VMEM((STEPS, 2, G, Z, C, T, RB), F32),
            pltpu.VMEM((STEPS, 2, SEQ, RB), BF16),
            pltpu.VMEM((STEPS, 2, SEQ, RB), BF16),
            pltpu.VMEM((STEPS, G, C, Z, T, RB), F32),
            pltpu.VMEM((STEPS, G, Z, T, RB), F32),
            pltpu.VMEM((STEPS, G, Z, T, RB), F32),
            pltpu.VMEM((2, C, G, HALF // C, RB), F32),
            pltpu.VMEM((X, G, HALF // C, RB), F32),
            pltpu.VMEM((G, HALF // C, 128), F32),
            pltpu.VMEM((STEPS, Z, 8, 128), F32),
            pltpu.VMEM((STEPS, Y, 8, 128), F32),
            pltpu.VMEM((STEPS, X * C, 8, 128), F32),
            pltpu.VMEM((G, Z, T, 128), F32),
            dma((5,)),
            dma((7,)), dma((Z,)),
            dma((2,)),
            dma((2,)), dma((2,)),
            dma((X, C)), dma((1,)),
            dma((STEPS, G, 2)), dma((STEPS, G, Y)),
            dma((STEPS, G)), dma((STEPS, G)),
            dma((STEPS, G)), dma((STEPS, G)),
            dma((STEPS, G)), dma((STEPS, G)),
            dma((STEPS, 3)), dma((STEPS, 3)),
        ],
        compiler_params=pltpu.CompilerParams(
            collective_id=0, has_side_effects=True, vmem_limit_bytes=52 * 1024 * 1024
        ),
    )(
        transition,
        alphas.reshape(STEPS, G, T, RB),
        beta_last.reshape(G, T, RB),
        emission,
        token_ids,
    )
    return beta.reshape(BS, RB), counts


def solution(mesh):
    return jax.shard_map(
        per_device,
        mesh=mesh,
        in_specs=(
            P("row", "col"),
            P(None, "col", "row"),
            P("col", "row"),
            P(None, "row"),
            P(None, "col"),
        ),
        out_specs=(P("col", "row"), P("row", "col")),
        check_vma=False,
    )
```

```python
import jax
import jax.numpy as jnp
from jax import lax
from jax.experimental import pallas as pl
from jax.experimental.pallas import tpu as pltpu
from jax.sharding import PartitionSpec as P

H = 16384
STEPS = 2
SEQ = 256
X, Y, Z, C = 4, 8, 8, 2
G = 2
BS = SEQ // (Z * C)
T = BS // G
HALF = SEQ // G
RB = H // (X * Y)
CB = H // (Z * C)
NCOL = 128
FACTOR = float(H * H) / float(SEQ * STEPS)
F32 = jnp.float32
BF16 = jnp.bfloat16
MESH = pl.DeviceIdType.MESH
NT = ((1,), (1,))
NN = ((1,), (0,))


def loop(n, body, start=0):
    def step(i, carry):
        body(i)
        return carry

    lax.fori_loop(start, n, step, 0)


def remote(src, dst, send, recv, row, col):
    return pltpu.make_async_remote_copy(
        src_ref=src, dst_ref=dst, send_sem=send, recv_sem=recv, device_id=(row, col), device_id_type=MESH
    )


def wait(ref, sem):
    pltpu.make_async_copy(ref, ref, sem).wait()


def near_first(j):
    return (j % 2) * ((j + 1) // 2) + (1 - j % 2) * (8 - j // 2)


def split(v):
    hi = v.astype(BF16)
    return hi, (v - hi.astype(F32)).astype(BF16)


def dot(a, b, dims):
    return lax.dot_general(a, b, (dims, ((), ())), preferred_element_type=F32)


def kernel(
    trans_hbm, alphas_hbm, beta_hbm, emis_hbm, tok_hbm,
    beta_out, counts_out,
    t_f, t_hi, t_lo, emis, beta0, tok, al, at, at_hi, at_lo, tsend, wblk, st, w, w_hi, w_lo, ub, pr, cr, g1, gx, zpart, zz, zy, zx, zc,
    ld, a_s, a_r, ap, b_s, b_r, g_s, g_r, y_s, y_r, x_s, x_r, p_s, p_r, c_s, c_r, z_s, z_r,
):
    row = lax.axis_index("row")
    col = lax.axis_index("col")
    x, y, z, k = row % X, row // X, col // C, col % C
    kd = x // 2
    slot = x % 2
    fslot = 1 - slot
    other = z * C + 1 - k

    bar = pltpu.get_barrier_semaphore()

    def greet(r, c):
        pl.semaphore_signal(bar, inc=1, device_id=(r, c), device_id_type=MESH)

    owner = 1 - (k + kd) % 2
    diag = 1 - ((y - z + Z) % Z + Z - 1) // Z

    def greet_cross(d):
        greet(((y + d) % Y) * X + x, y * C + k)
        greet(z * X + x, ((z + d) % Z) * C + k)

    def greet_lines(d):
        greet(row, ((z + d) % Z) * C + k)
        greet(((y + d) % Y) * X + x, col)

    def greet_x(d):
        greet(y * X + (x + d) % X, col)
        greet(y * X + (x + d) % X, other)

    loop(Z, greet_cross, 1)

    @pl.when(diag == 0)
    def _():
        greet(row, y * C + k)
        greet(z * X + x, col)

    loop(Z, greet_lines, 1)
    loop(X, greet_x, 1)
    greet(row, other)

    loads = [
        pltpu.make_async_copy(tok_hbm, tok, ld.at[0]),
        pltpu.make_async_copy(emis_hbm, emis, ld.at[1]),
        pltpu.make_async_copy(beta_hbm, beta0, ld.at[2]),
        pltpu.make_async_copy(alphas_hbm, al.at[:, :, k, z], ld.at[3]),
        pltpu.make_async_copy(trans_hbm, t_f, ld.at[4]),
    ]
    for c in loads:
        c.start()

    loads[0].wait()
    loads[1].wait()
    labels = lax.broadcasted_iota(jnp.int32, (NCOL, BS), 0)
    em = emis[...]

    def emit(step):
        onehot = (labels == tok[step : step + 1, :]).astype(F32)
        out = lax.dot_general(
            onehot, em, (((0,), (0,)), ((), ())), precision=lax.Precision.HIGHEST, preferred_element_type=F32
        )
        return out.reshape(G, T, RB)

    loads[2].wait()
    tsend[0] = emit(0) * beta0[...]

    pl.semaphore_wait(bar, 2 * (Z - 1) + 2 * (X - 1) + 1 + 2 * (Z - diag))

    def alpha_1_sends():
        ref = al.at[1, :, k, z]

        def send(j):
            remote(ref, ref, b_s.at[0], b_r.at[0], row, ((z + near_first(Z - j)) % Z) * C + k).start()

        loop(Z, send, 1)

    def alpha_1_on():
        wait(al.at[1, :, k, pl.ds(0, Z - 1)], b_r.at[0])
        half = al.at[1, :, k]
        remote(half, half, b_s.at[1], b_r.at[1], row, other).start()

    def alpha_step(i):
        if i < 4:
            b = (z - i + Z) % Z
            ref = al.at[0, :, k, b]
            if i:
                wait(ref, a_r.at[b])
            remote(ref, ref, a_s.at[i], a_r.at[b], row, ((z + 1) % Z) * C + k).start()
        if i < 3:
            b = (z + i) % Z
            ref = al.at[0, :, k, b]
            if i:
                wait(ref, a_r.at[b])
            remote(ref, ref, a_s.at[4 + i], a_r.at[b], row, ((z + Z - 1) % Z) * C + k).start()
        if i == 4:
            for b in ((z + 4) % Z, (z + 3) % Z):
                wait(al.at[0, :, k, b], a_r.at[b])
            half = al.at[0, :, k]
            remote(half, half, ap.at[0], ap.at[1], row, other).start()

    def y_sends(step, g, src):
        recv = y_r.at[step, g, z]

        def send_to(dst):
            def send(j):
                to = (y + near_first(Y - j)) % Y
                remote(src, dst, y_s.at[step, g, 0], recv, to * X + x, y * C + k).start()

            loop(Y, send, 1)

            @pl.when(diag == 1)
            def _():
                pltpu.make_async_copy(src, dst, recv).start()

            @pl.when(diag == 0)
            def _():
                remote(src, dst, y_s.at[step, g, 1], recv, row, y * C + k).start()

        @pl.when(owner == 1)
        def _():
            send_to(w.at[step, slot, g, z, k])

        @pl.when(owner == 0)
        def _():
            send_to(st.at[step, g, z])

    def x_stage(step, g, start=0, stop=Z // 2):
        def sends(here, block):
            def send(j):
                s = (z // 2 + (j % 2) * ((j + 1) // 2) + (1 - j % 2) * (4 - j // 2)) % 4 * 2
                for i in range(2):
                    wait(block(s + i), y_r.at[step, g, s + i])
                src = block(pl.ds(s, 2))
                dst = w.at[step, slot, g, pl.ds(s, 2), k]
                for d in (2, 1, 3):
                    remote(src, dst, x_s.at[step, g], x_r.at[step, g], y * X + (x + d) % X, z * C + kd).start()
                if here:
                    remote(src, dst, x_s.at[step, g], x_r.at[step, g], row, other).start()

            loop(stop, send, start)

        @pl.when(owner == 1)
        def _():
            sends(False, lambda s: w.at[step, slot, g, s, k])

        @pl.when(owner == 0)
        def _():
            sends(True, lambda s: st.at[step, g, s])

    def wait_x(step, g, sem):
        @pl.when(owner == 1)
        def _():
            wait(w.at[step, :, g, pl.ds(0, 3 * Z // 4)], sem)

        @pl.when(owner == 0)
        def _():
            wait(w.at[step, :, g], sem)

    def arrivals(step, g):
        wait_x(step, g, x_r.at[step, g])

    def product(step, g):
        acc = None
        for sl in range(2):
            hi, lo = split(jnp.concatenate([w[step, sl, g, :, c].reshape(HALF // C, RB) for c in range(C)], axis=0))
            w_hi[step, sl, g * HALF : (g + 1) * HALF, :] = hi
            w_lo[step, sl, g * HALF : (g + 1) * HALF, :] = lo
            cols = slice(sl * RB, (sl + 1) * RB)
            both = dot(jnp.concatenate([hi, lo], axis=0), t_hi[:, cols], NT)
            part = both[:HALF] + both[HALF:] + dot(hi, t_lo[:, cols], NT)
            acc = part if acc is None else acc + part
        ub[step, g] = acc.reshape(C, Z, T, RB)
        remote(ub.at[step, g, 1 - k], pr.at[step, g], p_s.at[step, g], p_r.at[step, g], row, other).start()

    def sums_out(step, g):
        wait(pr.at[step, g], p_r.at[step, g])
        ub[step, g, k] = ub[step, g, k] + pr[step, g]
        dst = cr.at[step, g, z]
        recv = c_r.at[step, g]

        def send(j):
            s = (z + near_first(Z - j)) % Z
            remote(ub.at[step, g, k, s], dst, c_s.at[step, g], recv, row, s * C + k).start()

        loop(Z, send, 1)
        pltpu.make_async_copy(ub.at[step, g, k, z], dst, recv).start()

    def reduced(step, g):
        wait(cr.at[step, g], c_r.at[step, g])
        acc = cr[step, g, 0]
        for i in range(1, Z):
            acc = acc + cr[step, g, i]
        return acc

    def next_weighted(g):
        wblk[g] = reduced(0, g) * tsend[1, g]
        y_sends(1, g, wblk.at[g])

    def lanes(parts):
        acc = None
        for v in parts:
            for i in range(RB // 128):
                t = v[:, i * 128 : (i + 1) * 128]
                acc = t if acc is None else acc + t
        return acc

    def z_part_0():
        v = (ub[0, :, k] * al[0, :, k]).reshape(SEQ // C, RB)
        zz[0, z] = z_row(lanes([v]))
        z_first(0)

    def z_row(part):
        return jnp.broadcast_to(jnp.sum(jnp.transpose(part), axis=0, keepdims=True), (8, SEQ // C))

    def z_first(step):
        if step:
            zz[1, z] = z_row(zpart[...].reshape(SEQ // C, 128))

        def send(d):
            ref = zz.at[step, z]
            remote(ref, ref, z_s.at[step, 0], z_r.at[step, 0], row, ((z + d) % Z) * C + k).start()

        loop(Z, send, 1)

    def alpha_transition():
        wait(al.at[1, :, 1 - k], b_r.at[1])
        n = HALF // C
        a_hi, a_lo = split(
            jnp.concatenate([al[1, g, c].reshape(n, RB) for c in range(C) for g in range(G)], axis=0)
        )
        for sl in range(2):
            cols = slice(sl * RB, (sl + 1) * RB)
            v = dot(a_hi, t_hi[:, cols], NN) + dot(a_lo, t_hi[:, cols], NN) + dot(a_hi, t_lo[:, cols], NN)
            g1[sl] = v.reshape(C, G, n, RB)

        for d in (2, 1, 3):
            to = (x + d) % X

            @pl.when(to // 2 == k)
            def _():
                for c in range(C):
                    remote(g1.at[to % 2, c], gx.at[x], g_s.at[d, c], g_r.at[0], y * X + to, z * C + c).start()

        @pl.when(owner == 1)
        def _():
            pltpu.make_async_copy(g1.at[slot, k], gx.at[x], g_r.at[0]).start()
            remote(g1.at[slot, 1 - k], gx.at[x], g_s.at[0, 0], g_r.at[0], row, other).start()

    def alpha_transition_sum():
        wait(gx, g_r.at[0])
        gx[0] = z_sum([gx[i] for i in range(X)])

    def z_part_1(g):
        n = HALF // C

        @pl.when(owner == 1)
        def _():
            zpart[g] = lanes([gx[0, g] * w[1, slot, g, :, k].reshape(n, RB)])

        @pl.when(owner == 0)
        def _():
            zpart[g] = lanes([gx[0, g] * st[1, g].reshape(n, RB)])

    def z_sum(parts):
        v = parts[0]
        for p in parts[1:]:
            v = v + p
        return v

    def z_second(step):
        wait(zz.at[step, pl.ds(0, Z - 1)], z_r.at[step, 0])
        zy[step, y] = z_sum([zz[step, i] for i in range(Z)])

        def send(d):
            ref = zy.at[step, y]
            remote(ref, ref, z_s.at[step, 1], z_r.at[step, 1], ((y + d) % Y) * X + x, col).start()

        loop(Y, send, 1)

    def z_third(step):
        wait(zy.at[step, pl.ds(0, Y - 1)], z_r.at[step, 1])
        zx[step, x * C + k] = z_sum([zy[step, i] for i in range(Y)])
        ref = zx.at[step, x * C + k]

        def send(d):
            remote(ref, ref, z_s.at[step, 2], z_r.at[step, 2], y * X + (x + d) % X, col).start()
            remote(ref, ref, z_s.at[step, 2], z_r.at[step, 2], y * X + (x + d) % X, other).start()

        loop(X, send, 1)
        remote(ref, ref, z_s.at[step, 2], z_r.at[step, 2], row, other).start()

    def z_last(step):
        wait(zx.at[step, pl.ds(0, X * C - 1)], z_r.at[step, 2])
        sums = [z_sum([zx[step, i * C + c, 0:1, :] for i in range(X)]) for c in range(C)]
        n = HALF // C
        inv = [1.0 / v for v in sums]
        scale = jnp.concatenate([v[:, g * n : (g + 1) * n] for g in range(G) for v in inv], axis=1)
        at_hi[...], at_lo[...] = split(at[step] * scale)

    def counts_part(step, sl):
        return (
            dot(at_hi[...], w_hi[step, sl], NN)
            + dot(at_lo[...], w_hi[step, sl], NN)
            + dot(at_hi[...], w_lo[step, sl], NN)
        )

    def alphas_turned():
        wait(al.at[0, :, 1 - k], ap.at[1])
        for step in range(STEPS):
            v = al[step].reshape(SEQ, RB)
            for i in range(RB // 128):
                at[step, i * 128 : (i + 1) * 128, :] = jnp.transpose(v[:, i * 128 : (i + 1) * 128])

    for g in range(G):
        y_sends(0, g, tsend.at[0, g])
    loads[3].wait()
    alpha_1_sends()
    tsend[1] = emit(1)

    loads[4].wait()

    def split_rows(i):
        r = pl.ds(pl.multiple_of(i * 64, 64), 64)
        hi, lo = split(t_f[r, :])
        t_hi[r, :] = hi
        t_lo[r, :] = lo

    loop(RB // 64, split_rows)

    x_stage(0, 0)
    alpha_step(0)
    x_stage(0, 1)
    alpha_1_on()
    arrivals(0, 0)
    product(0, 0)
    alpha_step(1)
    sums_out(0, 0)
    alpha_transition()
    arrivals(0, 1)
    product(0, 1)
    alpha_step(2)
    sums_out(0, 1)

    next_weighted(0)
    alpha_step(3)
    x_stage(1, 0, 0, 2)
    next_weighted(1)
    x_stage(1, 0, 2)
    alpha_step(4)
    z_part_0()
    x_stage(1, 1, 0, 2)
    alpha_transition_sum()
    z_part_1(0)
    x_stage(1, 1, 2)
    z_part_1(1)
    z_first(1)
    z_second(0)
    arrivals(1, 0)
    product(1, 0)
    sums_out(1, 0)
    alphas_turned()
    z_third(0)
    z_second(1)
    arrivals(1, 1)
    product(1, 1)
    sums_out(1, 1)
    z_third(1)

    z_last(0)
    for sl in range(2):
        counts_out[:, sl * RB : (sl + 1) * RB] = counts_part(0, sl)

    for step in range(STEPS):
        for g in range(G):
            wait(cr.at[step, g, pl.ds(0, Y - 1)], y_s.at[step, g, 0])
            wait(cr.at[step, g, pl.ds(0, Z - 1)], c_s.at[step, g])
            wait(pr.at[step, g], p_s.at[step, g])

            @pl.when(diag == 0)
            def _():
                wait(wblk.at[g], y_s.at[step, g, 1])

            wait_x(step, g, x_s.at[step, g])

        wait(zz.at[0, pl.ds(0, Z - 1)], z_s.at[step, 0])
        wait(zz.at[0, pl.ds(0, Y - 1)], z_s.at[step, 1])
        wait(zz.at[0, pl.ds(0, X * C - 1)], z_s.at[step, 2])

    for d in (1, 2, 3):
        @pl.when(((x + d) % X) // 2 == k)
        def _():
            for c in range(C):
                wait(gx.at[0], g_s.at[d, c])

    @pl.when(owner == 1)
    def _():
        wait(gx.at[0], g_s.at[0, 0])

    wait(al.at[1, :, k, pl.ds(0, Z - 1)], b_s.at[0])
    wait(al.at[1, :, k], b_s.at[1])
    for i in range(7):
        wait(al.at[0, :, 0, 0], a_s.at[i])
    wait(al.at[0, :, 0], ap.at[0])

    z_last(1)
    for sl in range(2):
        cols = slice(sl * RB, (sl + 1) * RB)
        counts_out[:, cols] = (t_f[:, cols] * (counts_out[:, cols] + counts_part(1, sl))) * FACTOR
    own = z_sum([zx[1, i * C + k, 0:1, :] for i in range(X)])
    zc[...] = jnp.transpose(jnp.broadcast_to(own, (128, SEQ // C))).reshape(G, Z, T, 128)
    for g in range(G):
        norm = zc[g, z]
        beta_out[g] = (reduced(1, g) / jnp.concatenate([norm] * (RB // 128), axis=1)) * float(H)


def per_device(transition, alphas, beta_last, emission, token_ids):
    hbm = pl.BlockSpec(memory_space=pltpu.HBM)
    vmem = pl.BlockSpec(memory_space=pltpu.VMEM)
    dma = pltpu.SemaphoreType.DMA
    beta, counts = pl.pallas_call(
        kernel,
        out_shape=(
            pltpu.VMEM((G, T, RB), F32),
            pltpu.VMEM((RB, CB), F32),
        ),
        in_specs=[hbm] * 5,
        out_specs=(vmem, vmem),
        scratch_shapes=[
            pltpu.VMEM((RB, CB), F32),
            pltpu.VMEM((RB, CB), BF16),
            pltpu.VMEM((RB, CB), BF16),
            pltpu.VMEM((NCOL, RB), F32),
            pltpu.VMEM((G, T, RB), F32),
            pltpu.VMEM((STEPS, BS), jnp.int32),
            pltpu.VMEM((STEPS, G, C, Z, T, RB), F32),
            pltpu.VMEM((STEPS, RB, SEQ), F32),
            pltpu.VMEM((RB, SEQ), BF16),
            pltpu.VMEM((RB, SEQ), BF16),
            pltpu.VMEM((2, G, T, RB), F32),
            pltpu.VMEM((G, T, RB), F32),
            pltpu.VMEM((STEPS, G, Z, T, RB), F32),
            pltpu.VMEM((STEPS, 2, G, Z, C, T, RB), F32),
            pltpu.VMEM((STEPS, 2, SEQ, RB), BF16),
            pltpu.VMEM((STEPS, 2, SEQ, RB), BF16),
            pltpu.VMEM((STEPS, G, C, Z, T, RB), F32),
            pltpu.VMEM((STEPS, G, Z, T, RB), F32),
            pltpu.VMEM((STEPS, G, Z, T, RB), F32),
            pltpu.VMEM((2, C, G, HALF // C, RB), F32),
            pltpu.VMEM((X, G, HALF // C, RB), F32),
            pltpu.VMEM((G, HALF // C, 128), F32),
            pltpu.VMEM((STEPS, Z, 8, 128), F32),
            pltpu.VMEM((STEPS, Y, 8, 128), F32),
            pltpu.VMEM((STEPS, X * C, 8, 128), F32),
            pltpu.VMEM((G, Z, T, 128), F32),
            dma((5,)),
            dma((7,)), dma((Z,)),
            dma((2,)),
            dma((2,)), dma((2,)),
            dma((X, C)), dma((1,)),
            dma((STEPS, G, 2)), dma((STEPS, G, Y)),
            dma((STEPS, G)), dma((STEPS, G)),
            dma((STEPS, G)), dma((STEPS, G)),
            dma((STEPS, G)), dma((STEPS, G)),
            dma((STEPS, 3)), dma((STEPS, 3)),
        ],
        compiler_params=pltpu.CompilerParams(
            collective_id=0, has_side_effects=True, vmem_limit_bytes=52 * 1024 * 1024
        ),
    )(
        transition,
        alphas.reshape(STEPS, G, T, RB),
        beta_last.reshape(G, T, RB),
        emission,
        token_ids,
    )
    return beta.reshape(BS, RB), counts


def solution(mesh):
    return jax.shard_map(
        per_device,
        mesh=mesh,
        in_specs=(
            P("row", "col"),
            P(None, "col", "row"),
            P("col", "row"),
            P(None, "row"),
            P(None, "col"),
        ),
        out_specs=(P("col", "row"), P("row", "col")),
        check_vma=False,
    )
```
